256 devices in a mesh: tile: 64 (over z_lo, x, y, core), mem: 4 (over z_hi).
Axes of the slice: x: 4, y: 4, z: 8 (z_hi: 4, z_lo: 2; z = z_hi * 2 + z_lo), core: 2. Of those that a mesh axis runs over, the one named last changes fastest.
Arguments:
- right_side: float32 [64, 256, 2048], P(None, 'tile'), may hold values from -6 to 6
- static_var: float32 [64, 256, 2048], P(None, 'tile'), may hold values from 0.3 to 3
- members: bfloat16 [20, 64, 1024, 128], P('mem', None, 'tile'), may hold values from -6 to 6
- vertical_root: float32 [64, 64], replicated, may hold values from -0.75 to 0.75
- stencil: int32 [512, 4], P('tile'), may hold values from 0 to 7
- weights: bfloat16 [4, 1024, 256], replicated, may hold values from -0.1875 to 0.1875
Outputs:
- solution_field: float32 [64, 256, 2048], P(None, 'tile')
- residual: float32 [64, 256, 2048], P(None, 'tile')
The draws below stay inside these ranges and needn't reach their ends.
Inputs may be any that keep to these rules, and one draw needn't show every extreme that they name: `stencil`: entries number fine blocks of the same index of tile, in the local order coarse row within the device times 4 plus segment.
All inputs are finite; a program needn't handle non-finite values.
Results may differ from the reference program's by a relative error of at most 0.0085.
Values may be sent and summed in bfloat16 or wider, within the bound.
A program may use at most 128 MiB of HBM per device.

```python
import math
import jax
import jax.numpy as jnp
from jax import lax

LEV = 64
COLS = 1024
BLOCK = 256
STENCIL = 4
REACH = 4
ITERS = 2
MEMBERS = 20
ROWS = 128
FINE_ROWS = 256
FINE_COLS = 2048
SEGMENTS = 4
BLOCKS_DEV = 8
BLOCKS = 512


def draw_right_side(key, part):
    key = jax.random.fold_in(key, 11)
    fraction = jnp.arange(FINE_ROWS, dtype=jnp.float32) / (FINE_ROWS - 1)
    scale_rows = 0.5 + fraction
    base = jnp.clip(jax.random.normal(key, (LEV, FINE_ROWS, FINE_COLS), jnp.float32), -4.0, 4.0)
    return base * scale_rows[None, :, None]


def touch_ends(array, own_key, low, top_value):
    index_at = [jax.random.randint(jax.random.fold_in(own_key, axis), (), 0, length) for axis, length in enumerate(array.shape)]
    longest = array.shape.index(max(array.shape))
    neighbour = index_at[:longest] + [(index_at[longest] + 1) % array.shape[longest]] + index_at[longest + 1:]
    return array.at[tuple(index_at)].set(low).at[tuple(neighbour)].set(top_value)


def block_levels(own_key, dims, pieces, smallest, largest):
    level = 1.0
    for dim, shards_of in pieces:
        draws = jax.random.uniform(jax.random.fold_in(jax.random.fold_in(own_key, 6), dim), (shards_of,), jnp.float32, smallest / len(pieces), largest / len(pieces))
        level = level * jnp.repeat(jnp.exp(draws), dims[dim] // shards_of).reshape((-1,) + (1,) * (len(dims) - 1 - dim))
    return level


def centred(own_key, extent, width, most, pieces=(), kind=jnp.bfloat16):
    factor_of = block_levels(own_key, extent, pieces, -0.22, 0.18) if pieces else 1.0
    drawn = jax.random.normal(own_key, extent, jnp.float32) * width * factor_of
    return jnp.minimum(jnp.maximum(drawn, -most), most).astype(kind)


def setup_inputs(seed: int = 0) -> dict:
    splits = jax.random.split(jax.random.key(seed), 7)
    return {
        "right_side": draw_right_side(jax.random.fold_in(splits[6], 71), 0),
        "static_var": jnp.clip(jnp.exp(math.log(3.0) - 2.3025851 * jax.random.uniform(splits[1], (LEV, FINE_ROWS, FINE_COLS), jnp.float32) ** block_levels(splits[1], (LEV, FINE_ROWS, FINE_COLS), ((1, 64),), -0.2, 0.2)), 0.3, 3.0),
        "members": centred(splits[2], (MEMBERS, LEV, COLS, ROWS), 1.0, 6.0, ((0, 4), (2, 64))),
        "vertical_root": centred(splits[3], (LEV, LEV), LEV ** -0.5, 0.75, (), jnp.float32),
        "stencil": touch_ends(jax.random.randint(splits[4], (BLOCKS, STENCIL), 0, BLOCKS_DEV), jax.random.fold_in(splits[4], 1), 0, BLOCKS_DEV - 1).astype(jnp.int32),
        "weights": centred(splits[5], (STENCIL, 4 * BLOCK, BLOCK), (4 * BLOCK) ** -0.5, 0.1875),
    }


def kernel_taps(reach):
    values = [math.exp(-(offset * offset) / (reach * reach)) for offset in range(-reach, reach + 1)]
    summed = sum(values)
    return [factor / summed for factor in values]


def fine_to_blocks(field_in, rows_count):
    levels = field_in.shape[0]
    segments = field_in.shape[2] // (2 * BLOCK)
    shaped = field_in.reshape(levels, rows_count, 2, segments, 2 * BLOCK)
    return shaped.transpose(1, 3, 0, 2, 4).reshape(rows_count * segments, levels, 4 * BLOCK)


def blocks_to_fine(blocks, rows_count, segments):
    levels = blocks.shape[1]
    shaped = blocks.reshape(rows_count, segments, levels, 2, 2 * BLOCK)
    return shaped.transpose(2, 0, 3, 1, 4).reshape(levels, 2 * rows_count, segments * 2 * BLOCK)


def coarse_to_grid(blocks, rows_count, segments):
    levels = blocks.shape[1]
    shaped = blocks.reshape(rows_count, segments, levels, BLOCK)
    return shaped.transpose(2, 1, 3, 0).reshape(levels, segments * BLOCK, rows_count)


def grid_to_coarse(grid, rows_count, segments):
    levels = grid.shape[0]
    shaped = grid.reshape(levels, segments, BLOCK, rows_count)
    return shaped.transpose(3, 1, 0, 2).reshape(rows_count * segments, levels, BLOCK)


def spread_field(data, kernel):
    reach = (len(kernel) - 1) // 2
    along_x = jnp.zeros(data.shape, jnp.float32)
    for offset in range(len(kernel)):
        along_x = along_x + kernel[offset] * jnp.roll(data, reach - offset, axis=1)
    padded = jnp.pad(along_x, ((0, 0), (0, 0), (reach, reach)))
    length = data.shape[2]
    along_y = jnp.zeros(data.shape, jnp.float32)
    for offset in range(len(kernel)):
        along_y = along_y + kernel[offset] * padded[:, :, offset:offset + length]
    return along_y


def ensemble_part(coarse_grid, members, vertical_root, kernel):
    coarse_float = coarse_grid.astype(jnp.float32)

    def member_term(running, member):
        member_float = member.astype(jnp.float32)
        weighted = member_float * coarse_float
        weighted = jnp.einsum('lk,lxy->kxy', vertical_root, weighted, precision=lax.Precision.HIGHEST)
        weighted = spread_field(spread_field(weighted, kernel), kernel)
        weighted = jnp.einsum('kl,lxy->kxy', vertical_root, weighted, precision=lax.Precision.HIGHEST)
        return running + member_float * weighted, None

    summed, unused = lax.scan(member_term, jnp.zeros(coarse_grid.shape, jnp.float32), members)
    return (summed / (MEMBERS - 1)).astype(jnp.bfloat16)


def apply_system(direction, static_var, members, vertical_root, stencil, weights, kernel):
    blocks = fine_to_blocks(direction.astype(jnp.bfloat16), ROWS)
    offsets = (jnp.arange(BLOCKS, dtype=jnp.int32) // BLOCKS_DEV) * BLOCKS_DEV
    coarse = jnp.zeros((BLOCKS, LEV, BLOCK), jnp.float32)
    for position in range(STENCIL):
        source = blocks[(stencil[:, position] + offsets).astype(jnp.int32)]
        coarse = coarse + jnp.einsum('blf,fc->blc', source.astype(jnp.float32), weights[position].astype(jnp.float32))
    coarse_grid = coarse_to_grid(coarse.astype(jnp.bfloat16), ROWS, SEGMENTS)
    ensemble = ensemble_part(coarse_grid, members, vertical_root, kernel)
    back = grid_to_coarse(ensemble, ROWS, SEGMENTS).astype(jnp.float32)
    fine_blocks = jnp.zeros((BLOCKS, LEV, 4 * BLOCK), jnp.float32)
    for position in range(STENCIL):
        update = jnp.einsum('blc,fc->blf', back, weights[position].astype(jnp.float32))
        fine_blocks = fine_blocks.at[(stencil[:, position] + offsets).astype(jnp.int32)].add(update)
    prolonged = blocks_to_fine(fine_blocks, ROWS, SEGMENTS)
    return direction + static_var * direction + prolonged


def reference(right_side, static_var, members, vertical_root, stencil, weights):
    kernel = kernel_taps(REACH)
    solution_field = jnp.zeros_like(right_side)
    residual = right_side
    direction = right_side
    norm_now = jnp.sum(residual * residual)
    for iteration in range(ITERS):
        product_image = apply_system(direction, static_var, members, vertical_root, stencil, weights, kernel)
        step_size = norm_now / jnp.sum(direction * product_image)
        solution_field = solution_field + step_size * direction
        residual = residual - step_size * product_image
        norm_next = jnp.sum(residual * residual)
        direction = residual + (norm_next / norm_now) * direction
        norm_now = norm_next
    return solution_field, residual
```

```python
import functools
import math

import jax
import jax.numpy as jnp
import numpy as np
from jax import lax
from jax.experimental import pallas as pl
from jax.experimental.pallas import tpu as pltpu
from jax.sharding import PartitionSpec as P

LEV = 64
COLS = 1024
BLOCK = 256
STENCIL = 4
REACH = 4
MEMBERS = 20
ROWS = 128
TILES = 64
MEMS = 4
LOCAL = 5
WIDTH = 16
QUARTER = TILES // MEMS
PAIRS = 32
MESH = pl.DeviceIdType.MESH
F32 = jnp.float32
BF16 = jnp.bfloat16


def kernel_taps(reach):
    values = [math.exp(-(offset * offset) / (reach * reach)) for offset in range(-reach, reach + 1)]
    summed = sum(values)
    return np.array([factor / summed for factor in values])


def row_operator():
    taps = kernel_taps(REACH)
    once = np.zeros((ROWS, ROWS))
    for row in range(ROWS):
        for offset in range(-REACH, REACH + 1):
            if 0 <= row + offset < ROWS:
                once[row, row + offset] = taps[offset + REACH]
    return once @ once


def row_blocks():
    twice = row_operator()
    kinds = []
    for group, shifts in ((8, range(-2, 3)), (0, range(0, 3)), (31, range(-2, 1))):
        for shift in shifts:
            at = 4 * (group + shift)
            kinds.append(twice[4 * group : 4 * group + 4, at : at + 4].T)
    return np.stack(kinds)


def column_operator():
    taps = kernel_taps(REACH)
    twice = np.convolve(taps, taps)
    places = list(range(WIDTH)) + list(range(-8, 0)) + list(range(WIDTH, WIDTH + 8))
    out = np.zeros((WIDTH, 2 * WIDTH))
    for to in range(WIDTH):
        for at, place in enumerate(places):
            if abs(place - to) <= 2 * REACH:
                out[to, at] = twice[place - to + 2 * REACH]
    return np.kron(np.eye(8), out)


def kernel(
    b_hbm, s_hbm, mem_hbm, amat_hbm, xop_hbm, st_ref, w_hbm, sol_hbm, res_hbm,
    bv, sv, ab, mem, amat, xop, wv, fb, onehot, send_c, recv_c, own_c, u, ens, es, rs, zs, back, hs, outv,
    part, sc1, sc2, sc3,
    load_sem, a_send, a_recv, b_send, b_recv, c_send, c_recv, s_send, s_recv, out_sem,
):
    me = lax.axis_index("tile")
    mm = lax.axis_index("mem")

    def at_tile(t):
        return {"tile": t, "mem": mm}

    def at_mem(m):
        return {"tile": me, "mem": m}

    barrier = pltpu.get_barrier_semaphore()

    def greet(k, carry):
        pl.semaphore_signal(barrier, inc=1, device_id=at_tile(lax.rem(me + k, TILES)), device_id_type=MESH)
        return carry

    lax.fori_loop(1, TILES, greet, 0)
    for k in range(1, MEMS):
        pl.semaphore_signal(barrier, inc=1, device_id=at_mem(lax.rem(mm + k, MEMS)), device_id_type=MESH)

    loads = []
    for r in range(4):
        loads.append(pltpu.make_async_copy(b_hbm.at[:, r, :], bv.at[r], load_sem.at[r]))
    loads.append(pltpu.make_async_copy(w_hbm, wv, load_sem.at[4]))
    for r in range(4):
        loads.append(pltpu.make_async_copy(s_hbm.at[:, r, :], sv.at[r], load_sem.at[5 + r]))
    loads.append(pltpu.make_async_copy(mem_hbm, mem, load_sem.at[9]))
    loads.append(pltpu.make_async_copy(amat_hbm, amat, load_sem.at[10]))
    loads.append(pltpu.make_async_copy(xop_hbm, xop, load_sem.at[11]))
    for load in loads:
        load.start()

    rows_at = lax.broadcasted_iota(jnp.int32, (LEV, 2 * LEV), 0)
    lanes_at = lax.broadcasted_iota(jnp.int32, (LEV, 2 * LEV), 1)
    eye0 = (lanes_at == rows_at).astype(F32)
    eye1 = (lanes_at == rows_at + LEV).astype(F32)
    for s in range(STENCIL):
        for q in range(4):
            e0 = st_ref[q, s]
            e1 = st_ref[4 + q, s]

            def place(j, carry, s=s, q=q, e0=e0, e1=e1):
                h0 = jnp.where(e0 == j, 1.0, 0.0).astype(F32)
                h1 = jnp.where(e1 == j, 1.0, 0.0).astype(F32)
                onehot[pl.ds(pl.multiple_of((s * 8 + j) * LEV, LEV), LEV), q * 128 : q * 128 + 128] = (
                    eye0 * h0 + eye1 * h1
                ).astype(BF16)
                return carry

            lax.fori_loop(0, 8, place, 0)
    for m in range(LOCAL):
        u[m, 0:32, :] = jnp.zeros((32, 256), BF16)
        u[m, 544:576, :] = jnp.zeros((32, 256), BF16)

    def pack_row(v):
        return jnp.sum(v.reshape(-1, 8, 128), axis=0).sum(axis=0, keepdims=True)

    def restrict(it):
        acc = None
        for s in range(STENCIL):
            rows = []
            for q in range(4):
                for i in range(2):
                    rows.append(fb[st_ref[4 * i + q, s]])
            term = jnp.dot(jnp.concatenate(rows, axis=0), wv[s], preferred_element_type=F32)
            acc = term if acc is None else acc + term
        for q in range(4):
            turned = acc[q * 128 : q * 128 + 128].T
            own_c[q * 256 : q * 256 + 256, :] = turned
        grid = own_c[...].reshape(TILES, 2, 8, 128)
        first, last = grid[:, 0], grid[:, 1]
        before = jnp.concatenate([last[TILES - 1 :], last[: TILES - 1]], axis=0)
        after = jnp.concatenate([first[1:], first[:1]], axis=0)
        send_c[it, :, 0:16, :] = jnp.concatenate([first, last], axis=1).astype(BF16)
        send_c[it, :, 16:32, :] = jnp.concatenate([before, after], axis=1).astype(BF16)

    def fill_blocks(r, field):
        p, rr = r // 2, r % 2
        for q in range(4):
            fb[4 * p + q, :, rr * 512 : rr * 512 + 512] = field[:, q * 512 : q * 512 + 512]

    mine = lax.rem(me, 2) * PAIRS + lax.div(me, 2)

    def wait_bytes(ref, sem):
        pltpu.make_async_copy(ref, ref, sem).wait()

    def c_copy(it, t):
        return pltpu.make_async_remote_copy(
            src_ref=send_c.at[it, t],
            dst_ref=recv_c.at[it, mine],
            send_sem=a_send.at[it],
            recv_sem=a_recv.at[it],
            device_id=at_tile(t),
            device_id_type=MESH,
        )

    def start_c(it):
        def go(k, carry):
            c_copy(it, lax.rem(me + k, TILES)).start()
            return carry

        lax.fori_loop(1, TILES, go, 0)
        recv_c[it, mine] = send_c[it, me]

    def wait_c(it):
        wait_bytes(recv_c.at[it, 0 : TILES - 1], a_recv.at[it])
        wait_bytes(send_c.at[it, 0 : TILES - 1], a_send.at[it])

    low = lax.rem(me, 8)
    high = lax.div(me, 8)

    def sum_copy(x, stage, k):
        if stage == 0:
            slot, dst = low, sc1
            to = at_tile(high * 8 + lax.rem(low + k, 8))
        elif stage == 1:
            slot, dst = high, sc2
            to = at_tile(lax.rem(high + k, 8) * 8 + low)
        else:
            slot, dst = mm, sc3
            to = at_mem(lax.rem(mm + k, MEMS))
        return pltpu.make_async_remote_copy(
            src_ref=part.at[x, stage],
            dst_ref=dst.at[x, slot],
            send_sem=s_send.at[x, stage],
            recv_sem=s_recv.at[x, stage],
            device_id=to,
            device_id_type=MESH,
        )

    def sum_start(x, stage, value):
        part[x, stage] = value
        if stage == 0:
            sc1[x, low] = value
        elif stage == 1:
            sc2[x, high] = value
        else:
            sc3[x, mm] = value

        def go(k, carry):
            sum_copy(x, stage, k).start()
            return carry

        lax.fori_loop(1, MEMS if stage == 2 else 8, go, 0)

    def sum_end(x, stage):
        held = (sc1, sc2, sc3)[stage]
        count = MEMS - 1 if stage == 2 else 7
        wait_bytes(held.at[x, 0:count], s_recv.at[x, stage])
        wait_bytes(held.at[x, 0:count], s_send.at[x, stage])
        return jnp.sum(held[x], axis=0)

    def stack_rows(rows):
        rows = rows + [jnp.zeros((8 - len(rows), 128), F32)]
        return jnp.concatenate(rows, axis=0)

    def pick(tile, row):
        return jnp.sum(tile[row : row + 1, :], axis=1, keepdims=True)

    def ensemble(it):
        def member(m, carry):
            for g in range(4):
                lanes = []
                for par in range(2):
                    w = mem[m, par, 8 * g : 8 * g + 8] * recv_c[it, par * PAIRS + 8 * g : par * PAIRS + 8 * g + 8]
                    lanes.append(w.reshape(256, 128))
                mixed = jnp.dot(xop[...], jnp.concatenate(lanes, axis=1), preferred_element_type=F32)
                u[m, 32 + 128 * g : 160 + 128 * g, :] = mixed.astype(BF16)
            for g in range(4):
                at = 32 + 128 * g
                wide = jnp.concatenate([u[m, at + 16 * d : at + 16 * d + 128, :] for d in range(-2, 3)], axis=1)
                inner = jnp.dot(wide, amat[0:1280, :], preferred_element_type=F32)
                if g == 0:
                    edge = jnp.concatenate([u[m, 32 + 16 * d : 48 + 16 * d, :] for d in range(0, 3)], axis=1)
                    edge = jnp.dot(edge, amat[1280:2048, :], preferred_element_type=F32)
                    inner = jnp.concatenate([edge, inner[16:]], axis=0)
                if g == 3:
                    edge = jnp.concatenate([u[m, 528 + 16 * d : 544 + 16 * d, :] for d in range(-2, 1)], axis=1)
                    edge = jnp.dot(edge, amat[2048:2816, :], preferred_element_type=F32)
                    inner = jnp.concatenate([inner[:112], edge], axis=0)
                for par in range(2):
                    own = mem[m, par, 8 * g : 8 * g + 8, 0:16, :].astype(F32)
                    term = own * inner[:, par * 128 : par * 128 + 128].reshape(8, 16, 128)
                    ens[par, 8 * g : 8 * g + 8] += term
            return carry

        ens[...] = jnp.zeros_like(ens)
        lax.fori_loop(0, LOCAL, member, 0)
        es[it] = jnp.stack([ens[0], ens[1]], axis=1).reshape(TILES, 16, 128).astype(BF16)

    def rs_copy(it, k):
        to = lax.rem(mm + k, MEMS)
        return pltpu.make_async_remote_copy(
            src_ref=es.at[it, pl.ds(to * QUARTER, QUARTER)],
            dst_ref=rs.at[it, mm],
            send_sem=b_send.at[it],
            recv_sem=b_recv.at[it],
            device_id=at_mem(to),
            device_id_type=MESH,
        )

    def start_rs(it):
        for k in (2, 1, 3):
            rs_copy(it, k).start()
        rs[it, mm] = es[it, pl.ds(mm * QUARTER, QUARTER)]

    def wait_rs(it):
        wait_bytes(rs.at[it, 0 : MEMS - 1], b_recv.at[it])
        wait_bytes(rs.at[it, 0 : MEMS - 1], b_send.at[it])
        total = rs[it, 0].astype(F32)
        for m in range(1, MEMS):
            total = total + rs[it, m].astype(F32)
        zs[it] = total.astype(BF16)

    def back_copy(it, tt, m):
        return pltpu.make_async_remote_copy(
            src_ref=zs.at[it, tt],
            dst_ref=back.at[it, me],
            send_sem=c_send.at[it],
            recv_sem=c_recv.at[it],
            device_id={"tile": mm * QUARTER + tt, "mem": m},
            device_id_type=MESH,
        )

    def start_back(it):
        def go(k, carry):
            m = lax.rem(mm + lax.div(k, QUARTER), MEMS)
            tt = lax.rem(me + k, QUARTER)
            itself = jnp.logical_and(mm * QUARTER + tt == me, m == mm)

            @pl.when(jnp.logical_not(itself))
            def _():
                back_copy(it, tt, m).start()

            @pl.when(itself)
            def _():
                pltpu.make_async_copy(zs.at[it, tt], back.at[it, me], c_recv.at[it]).start()

            return carry

        lax.fori_loop(0, TILES, go, 0)

    def wait_back(it):
        wait_bytes(back.at[it], c_recv.at[it])
        to_self = lax.div(me, QUARTER) == mm

        @pl.when(to_self)
        def _():
            wait_bytes(back.at[it, 0 : TILES - 1], c_send.at[it])

        @pl.when(jnp.logical_not(to_self))
        def _():
            wait_bytes(back.at[it], c_send.at[it])

    def gather_back(it):
        wide = jnp.concatenate([back[it, 16 * q : 16 * q + 16].reshape(256, 128) for q in range(4)], axis=1)
        for s in range(STENCIL):
            hs[s] = lax.dot_general(
                onehot[s * 512 : s * 512 + 512, :], wide, (((1,), (1,)), ((), ())), preferred_element_type=F32
            ).astype(BF16)

    def prolong(piece):
        total = None
        for s in range(STENCIL):
            term = lax.dot_general(
                hs[s],
                wv[s, piece * 256 : piece * 256 + 256, :],
                (((1,), (1,)), ((), ())),
                preferred_element_type=F32,
            )
            total = term if total is None else total + term
        return total

    for r in range(4):
        loads[r].wait()
        fill_blocks(r, bv[r].astype(BF16))
    loads[4].wait()
    restrict(0)
    pl.semaphore_wait(barrier, TILES - 1 + MEMS - 1)
    start_c(0)
    for r in range(4):
        loads[5 + r].wait()
    square = jnp.zeros((1, 128), F32)
    diag = jnp.zeros((1, 128), F32)
    for r in range(4):
        v = bv[r]
        square = square + pack_row(v * v)
        diag = diag + pack_row(v * v * (1.0 + sv[r]))
    sum_start(0, 0, stack_rows([square, diag]))
    for load in loads[9:]:
        load.wait()
    sum_start(0, 1, sum_end(0, 0))
    first_sums = sum_end(0, 1)
    wait_c(0)
    ensemble(0)
    start_rs(0)

    def col_dot(c_it):
        v = jnp.zeros((1, 128), F32)
        for par in range(2):
            v = v + pack_row(ens[par] * recv_c[c_it, par * PAIRS : par * PAIRS + PAIRS, 0:16, :].astype(F32))
        return v

    sum_start(1, 0, stack_rows([col_dot(0)]))
    wait_rs(0)
    start_back(0)
    sum_start(1, 1, sum_end(1, 0))
    sum_start(1, 2, sum_end(1, 1))
    second_sums = sum_end(1, 2)
    rr = pick(first_sums, 0)
    dad = pick(first_sums, 1) + pick(second_sums, 0)
    alpha = rr / dad
    wait_back(0)
    gather_back(0)
    square = jnp.zeros((1, 128), F32)
    diag = jnp.zeros((1, 128), F32)
    cross = jnp.zeros((1, 128), F32)
    for piece in range(4):
        rr_, half = piece // 2, piece % 2
        total = prolong(piece)
        for p in range(2):
            for q in range(4):
                r = 2 * p + rr_
                cols = slice(q * 512 + half * 256, q * 512 + half * 256 + 256)
                j = 4 * p + q
                d = bv[r, :, cols]
                factor = 1.0 + sv[r, :, cols]
                image = d * factor + total[j * 64 : j * 64 + 64, :]
                ab[r, :, cols] = image
                rnew = d - alpha * image
                fb[j, :, piece * 256 : piece * 256 + 256] = rnew.astype(BF16)
                square = square + pack_row(rnew * rnew)
                diag = diag + pack_row(rnew * rnew * factor)
                cross = cross + pack_row(d * rnew * factor)
    restrict(1)
    start_c(1)
    sum_start(2, 0, stack_rows([square, diag, cross]))
    sum_start(2, 1, sum_end(2, 0))
    third_sums = sum_end(2, 1)
    wait_c(1)
    ensemble(1)
    start_rs(1)
    sum_start(3, 0, stack_rows([col_dot(1), col_dot(0)]))
    wait_rs(1)
    start_back(1)
    sum_start(3, 1, sum_end(3, 0))
    sum_start(3, 2, sum_end(3, 1))
    fourth_sums = sum_end(3, 2)
    new = pick(third_sums, 0)
    beta = new / rr
    both = pick(third_sums, 2) + pick(fourth_sums, 1)
    dad2 = pick(third_sums, 1) + pick(fourth_sums, 0) + 2.0 * beta * both + beta * beta * dad
    alpha2 = new / dad2
    wait_back(1)
    gather_back(1)
    for piece in range(4):
        rr_, half = piece // 2, piece % 2
        total = prolong(piece)
        for p in range(2):
            for q in range(4):
                r = 2 * p + rr_
                cols = slice(q * 512 + half * 256, q * 512 + half * 256 + 256)
                j = 4 * p + q
                d = bv[r, :, cols]
                image = ab[r, :, cols]
                rnew = d - alpha * image
                second = rnew * (1.0 + sv[r, :, cols]) + total[j * 64 : j * 64 + 64, :] + beta * image
                outv[0, r, :, cols] = alpha * d + alpha2 * (rnew + beta * d)
                outv[1, r, :, cols] = rnew - alpha2 * second
    stores = []
    for r in range(4):
        stores.append(pltpu.make_async_copy(outv.at[0, r], sol_hbm.at[:, r, :], out_sem.at[r]))
        stores.append(pltpu.make_async_copy(outv.at[1, r], res_hbm.at[:, r, :], out_sem.at[4 + r]))
    for store in stores:
        store.start()
    for store in stores:
        store.wait()


def on_device(right_side, static_var, members, vertical_root, stencil, weights):
    turned = members.reshape(LOCAL, LEV, WIDTH, PAIRS, 2, 2).transpose(0, 4, 3, 2, 5, 1)
    turned = turned.reshape(LOCAL, 2, PAIRS, WIDTH, 128)
    up = [(i, (i + 1) % TILES) for i in range(TILES)]
    down = [(j, i) for i, j in up]
    before = lax.ppermute(turned[:, :, :, 8:], "tile", up)
    after = lax.ppermute(turned[:, :, :, :8], "tile", down)
    extended = jnp.concatenate([turned, before, after], axis=3)
    both = jnp.einsum("kl,jl->kj", vertical_root, vertical_root, precision=lax.Precision.HIGHEST)
    both = both / (MEMBERS - 1)
    blocks = jnp.asarray(row_blocks(), F32)
    amat = (blocks[:, :, None, :, None] * both[None, None, :, None, :]).reshape(11 * 256, 256).astype(BF16)
    xop = jnp.asarray(column_operator(), BF16)
    anyspec = pl.BlockSpec(memory_space=pl.ANY)
    field = jax.ShapeDtypeStruct(right_side.shape, F32)
    return pl.pallas_call(
        kernel,
        out_shape=(field, field),
        in_specs=[anyspec] * 5 + [pl.BlockSpec(memory_space=pltpu.SMEM), anyspec],
        out_specs=(anyspec, anyspec),
        scratch_shapes=[
            pltpu.VMEM((4, LEV, 2048), F32),
            pltpu.VMEM((4, LEV, 2048), F32),
            pltpu.VMEM((4, LEV, 2048), F32),
            pltpu.VMEM((LOCAL, 2, PAIRS, 32, 128), BF16),
            pltpu.VMEM((11 * 256, 256), BF16),
            pltpu.VMEM((128, 256), BF16),
            pltpu.VMEM((STENCIL, 1024, 256), BF16),
            pltpu.VMEM((8, LEV, 1024), BF16),
            pltpu.VMEM((2048, 512), BF16),
            pltpu.VMEM((2, TILES, 32, 128), BF16),
            pltpu.VMEM((2, TILES, 32, 128), BF16),
            pltpu.VMEM((COLS, 128), F32),
            pltpu.VMEM((LOCAL, 576, 256), BF16),
            pltpu.VMEM((2, PAIRS, 16, 128), F32),
            pltpu.VMEM((2, TILES, 16, 128), BF16),
            pltpu.VMEM((2, MEMS, QUARTER, 16, 128), BF16),
            pltpu.VMEM((2, QUARTER, 16, 128), BF16),
            pltpu.VMEM((2, TILES, 16, 128), BF16),
            pltpu.VMEM((STENCIL, 512, 256), BF16),
            pltpu.VMEM((2, 4, LEV, 2048), F32),
            pltpu.VMEM((4, 3, 8, 128), F32),
            pltpu.VMEM((4, 8, 8, 128), F32),
            pltpu.VMEM((4, 8, 8, 128), F32),
            pltpu.VMEM((4, MEMS, 8, 128), F32),
            pltpu.SemaphoreType.DMA((12,)),
            pltpu.SemaphoreType.DMA((2,)),
            pltpu.SemaphoreType.DMA((2,)),
            pltpu.SemaphoreType.DMA((2,)),
            pltpu.SemaphoreType.DMA((2,)),
            pltpu.SemaphoreType.DMA((2,)),
            pltpu.SemaphoreType.DMA((2,)),
            pltpu.SemaphoreType.DMA((4, 3)),
            pltpu.SemaphoreType.DMA((4, 3)),
            pltpu.SemaphoreType.DMA((8,)),
        ],
        compiler_params=pltpu.CompilerParams(
            collective_id=0, has_side_effects=True, vmem_limit_bytes=56 * 1024 * 1024
        ),
        name="conjugate_gradient",
    )(right_side, static_var, extended, amat, xop, stencil, weights)


def solution(mesh):
    in_specs = (
        P(None, "tile", None),
        P(None, "tile", None),
        P("mem", None, "tile", None),
        P(),
        P("tile", None),
        P(),
    )
    out_specs = (P(None, "tile", None), P(None, "tile", None))
    return jax.shard_map(on_device, mesh=mesh, in_specs=in_specs, out_specs=out_specs, check_vma=False)
```

```python
import functools
import math

import jax
import jax.numpy as jnp
import numpy as np
from jax import lax
from jax.experimental import pallas as pl
from jax.experimental.pallas import tpu as pltpu
from jax.sharding import PartitionSpec as P

LEV = 64
COLS = 1024
BLOCK = 256
STENCIL = 4
REACH = 4
MEMBERS = 20
ROWS = 128
TILES = 64
MEMS = 4
LOCAL = 5
WIDTH = 16
QUARTER = TILES // MEMS
PAIRS = 32
MESH = pl.DeviceIdType.MESH
F32 = jnp.float32
BF16 = jnp.bfloat16


def kernel_taps(reach):
    values = [math.exp(-(offset * offset) / (reach * reach)) for offset in range(-reach, reach + 1)]
    summed = sum(values)
    return np.array([factor / summed for factor in values])


def row_operator():
    taps = kernel_taps(REACH)
    once = np.zeros((ROWS, ROWS))
    for row in range(ROWS):
        for offset in range(-REACH, REACH + 1):
            if 0 <= row + offset < ROWS:
                once[row, row + offset] = taps[offset + REACH]
    return once @ once


def row_blocks():
    twice = row_operator()
    kinds = []
    for group, shifts in ((8, range(-2, 3)), (0, range(0, 3)), (31, range(-2, 1))):
        for shift in shifts:
            at = 4 * (group + shift)
            kinds.append(twice[4 * group : 4 * group + 4, at : at + 4].T)
    return np.stack(kinds)


def column_operator():
    taps = kernel_taps(REACH)
    twice = np.convolve(taps, taps)
    places = list(range(WIDTH)) + list(range(-8, 0)) + list(range(WIDTH, WIDTH + 8))
    out = np.zeros((WIDTH, 2 * WIDTH))
    for to in range(WIDTH):
        for at, place in enumerate(places):
            if abs(place - to) <= 2 * REACH:
                out[to, at] = twice[place - to + 2 * REACH]
    return np.kron(np.eye(8), out)


def kernel(
    b_hbm, s_hbm, mem_hbm, root_ref, coef_ref, xop, perm, st_ref, w_hbm, sol_hbm, res_hbm,
    bv, sv, ab, mraw, wide_t, wide_g, halo_send, halo_recv, mem, amat, wv, fb, onehot, send_c, recv_c, own_c, u, ens, es, rs, zs, back, hs, outv,
    part, sc1, sc2, sc3,
    load_sem, a_send, a_recv, b_send, b_recv, c_send, c_recv, s_send, s_recv, h_send, h_recv, out_sem,
):
    me = lax.axis_index("tile")
    mm = lax.axis_index("mem")

    def wait_bytes(ref, sem):
        pltpu.make_async_copy(ref, ref, sem).wait()

    def at_tile(t):
        return {"tile": t, "mem": mm}

    def at_mem(m):
        return {"tile": me, "mem": m}

    barrier = pltpu.get_barrier_semaphore()

    def greet(k, carry):
        pl.semaphore_signal(barrier, inc=1, device_id=at_tile(lax.rem(me + k, TILES)), device_id_type=MESH)
        return carry

    lax.fori_loop(1, TILES, greet, 0)
    for k in range(1, MEMS):
        pl.semaphore_signal(barrier, inc=1, device_id=at_mem(lax.rem(mm + k, MEMS)), device_id_type=MESH)

    loads = []
    for r in range(4):
        loads.append(pltpu.make_async_copy(b_hbm.at[:, r, :], bv.at[r], load_sem.at[r]))
    loads.append(pltpu.make_async_copy(w_hbm, wv, load_sem.at[4]))
    for r in range(4):
        loads.append(pltpu.make_async_copy(s_hbm.at[:, r, :], sv.at[r], load_sem.at[5 + r]))
    loads.append(pltpu.make_async_copy(mem_hbm, mraw, load_sem.at[9]))
    for load in loads:
        load.start()

    def build():
        rows_at = lax.broadcasted_iota(jnp.int32, (LEV, 2 * LEV), 0)
        lanes_at = lax.broadcasted_iota(jnp.int32, (LEV, 2 * LEV), 1)
        eye0 = (lanes_at == rows_at).astype(F32)
        eye1 = (lanes_at == rows_at + LEV).astype(F32)
        for s in range(STENCIL):
            for q in range(4):
                e0 = st_ref[q, s]
                e1 = st_ref[4 + q, s]

                def place(j, carry, s=s, q=q, e0=e0, e1=e1):
                    h0 = jnp.where(e0 == j, 1.0, 0.0).astype(F32)
                    h1 = jnp.where(e1 == j, 1.0, 0.0).astype(F32)
                    onehot[pl.ds(pl.multiple_of((s * 8 + j) * LEV, LEV), LEV), q * 128 : q * 128 + 128] = (
                        eye0 * h0 + eye1 * h1
                    ).astype(BF16)
                    return carry

                lax.fori_loop(0, 8, place, 0)
        for m in range(LOCAL):
            u[m, 0:32, :] = jnp.zeros((32, 256), BF16)
            u[m, 544:576, :] = jnp.zeros((32, 256), BF16)
        both = lax.dot_general(
            root_ref[...],
            root_ref[...],
            (((1,), (1,)), ((), ())),
            preferred_element_type=F32,
            precision=lax.Precision.HIGHEST,
        ) * (1.0 / (MEMBERS - 1))
        four = jnp.concatenate([both] * 4, axis=1)

        def scale(n, carry):
            amat[pl.ds(pl.multiple_of(n * LEV, LEV), LEV), :] = (four * coef_ref[pl.ds(n, 1), :]).astype(BF16)
            return carry

        lax.fori_loop(0, 44, scale, 0)

    def halo_copy(side, m):
        to = lax.rem(me + (TILES - 1 if side == 0 else 1), TILES)
        return pltpu.make_async_remote_copy(
            src_ref=halo_send.at[side, m],
            dst_ref=halo_recv.at[side, m],
            send_sem=h_send.at[side],
            recv_sem=h_recv.at[side],
            device_id=at_tile(to),
            device_id_type=MESH,
        )

    def turn(m, carry):
        wide_t[...] = mraw[m].reshape(COLS, 128).astype(F32)
        for c in range(WIDTH):
            at = wide_t[pl.ds(c, LEV, stride=WIDTH), :].astype(BF16)
            rows = lax.dot_general(perm[...], at, (((1,), (1,)), ((), ())), preferred_element_type=F32)
            wide_g[pl.ds(c, TILES, stride=WIDTH), :] = jnp.concatenate([rows[:64], rows[64:]], axis=1)
        turned = wide_g[...]
        mem[m, :, 0:16, :] = turned.reshape(TILES, 16, 128).astype(BF16)
        halves = turned.reshape(TILES, 2, 8, 128)
        for side in range(2):
            halo_send[side, m] = halves[:, side].reshape(PAIRS, 16, 128).astype(BF16)
            halo_copy(side, m).start()
        return carry

    def wait_halo():
        for side in range(2):
            wait_bytes(halo_recv.at[side], h_recv.at[side])
            wait_bytes(halo_send.at[side], h_send.at[side])

        def join(m, carry):
            before = halo_recv[1, m].astype(F32).reshape(TILES, 8, 128)
            after = halo_recv[0, m].astype(F32).reshape(TILES, 8, 128)
            mem[m, :, 16:32, :] = jnp.concatenate([before, after], axis=1).astype(BF16)
            return carry

        lax.fori_loop(0, LOCAL, join, 0)

    def pack_row(v):
        return jnp.sum(v.reshape(-1, 8, 128), axis=0).sum(axis=0, keepdims=True)

    def restrict(it):
        acc = None
        for s in range(STENCIL):
            rows = []
            for q in range(4):
                for i in range(2):
                    rows.append(fb[st_ref[4 * i + q, s]])
            term = jnp.dot(jnp.concatenate(rows, axis=0), wv[s], preferred_element_type=F32)
            acc = term if acc is None else acc + term
        for q in range(4):
            turned = acc[q * 128 : q * 128 + 128].T
            own_c[q * 256 : q * 256 + 256, :] = turned
        grid = own_c[...].reshape(TILES, 2, 8, 128)
        first, last = grid[:, 0], grid[:, 1]
        before = jnp.concatenate([last[TILES - 1 :], last[: TILES - 1]], axis=0)
        after = jnp.concatenate([first[1:], first[:1]], axis=0)
        send_c[it, :, 0:16, :] = jnp.concatenate([first, last], axis=1).astype(BF16)
        send_c[it, :, 16:32, :] = jnp.concatenate([before, after], axis=1).astype(BF16)

    def fill_blocks(r, field):
        p, rr = r // 2, r % 2
        for q in range(4):
            fb[4 * p + q, :, rr * 512 : rr * 512 + 512] = field[:, q * 512 : q * 512 + 512]

    mine = lax.rem(me, 2) * PAIRS + lax.div(me, 2)


    def c_copy(it, t):
        return pltpu.make_async_remote_copy(
            src_ref=send_c.at[it, t],
            dst_ref=recv_c.at[it, mine],
            send_sem=a_send.at[it],
            recv_sem=a_recv.at[it],
            device_id=at_tile(t),
            device_id_type=MESH,
        )

    def start_c(it):
        def go(k, carry):
            c_copy(it, lax.rem(me + k, TILES)).start()
            return carry

        lax.fori_loop(1, TILES, go, 0)
        recv_c[it, mine] = send_c[it, me]

    def wait_c(it):
        wait_bytes(recv_c.at[it, 0 : TILES - 1], a_recv.at[it])
        wait_bytes(send_c.at[it, 0 : TILES - 1], a_send.at[it])

    low = lax.rem(me, 8)
    high = lax.div(me, 8)

    def sum_copy(x, stage, k):
        if stage == 0:
            slot, dst = low, sc1
            to = at_tile(high * 8 + lax.rem(low + k, 8))
        elif stage == 1:
            slot, dst = high, sc2
            to = at_tile(lax.rem(high + k, 8) * 8 + low)
        else:
            slot, dst = mm, sc3
            to = at_mem(lax.rem(mm + k, MEMS))
        return pltpu.make_async_remote_copy(
            src_ref=part.at[x, stage],
            dst_ref=dst.at[x, slot],
            send_sem=s_send.at[x, stage],
            recv_sem=s_recv.at[x, stage],
            device_id=to,
            device_id_type=MESH,
        )

    def sum_start(x, stage, value):
        part[x, stage] = value
        if stage == 0:
            sc1[x, low] = value
        elif stage == 1:
            sc2[x, high] = value
        else:
            sc3[x, mm] = value

        def go(k, carry):
            sum_copy(x, stage, k).start()
            return carry

        lax.fori_loop(1, MEMS if stage == 2 else 8, go, 0)

    def sum_end(x, stage):
        held = (sc1, sc2, sc3)[stage]
        count = MEMS - 1 if stage == 2 else 7
        wait_bytes(held.at[x, 0:count], s_recv.at[x, stage])
        wait_bytes(held.at[x, 0:count], s_send.at[x, stage])
        return jnp.sum(held[x], axis=0)

    def stack_rows(rows):
        rows = rows + [jnp.zeros((8 - len(rows), 128), F32)]
        return jnp.concatenate(rows, axis=0)

    def pick(tile, row):
        return jnp.sum(tile[row : row + 1, :], axis=1, keepdims=True)

    def mix(it):
        def member(m, carry):
            for g in range(4):
                lanes = []
                for par in range(2):
                    at = par * PAIRS + 8 * g
                    lanes.append((mem[m, at : at + 8] * recv_c[it, at : at + 8]).reshape(256, 128))
                mixed = jnp.dot(xop[...], jnp.concatenate(lanes, axis=1), preferred_element_type=F32)
                u[m, 32 + 128 * g : 160 + 128 * g, :] = mixed.astype(BF16)
            return carry

        lax.fori_loop(0, LOCAL, member, 0)

    def own_part(m, at, count):
        return mem[m, pl.ds(at, count), 0:16, :].astype(F32)

    def ensemble(it):
        mix(it)

        def group(turn_at, carry):
            k = jnp.where(turn_at == 0, 2, jnp.where(turn_at == 1, 1, jnp.where(turn_at == 2, 3, 0)))
            g = lax.rem(mm + k, MEMS)
            wide = []
            for m in range(LOCAL):
                pieces = []
                for d in range(-2, 3):
                    pieces.append(u[m, pl.ds(pl.multiple_of(32 + 128 * g + 16 * d, 16), 128), :])
                wide.append(jnp.concatenate(pieces, axis=1))
            inner = jnp.dot(jnp.concatenate(wide, axis=0), amat[0:1280, :], preferred_element_type=F32)
            for par in range(2):
                total = jnp.zeros((8, 16, 128), F32)
                for m in range(LOCAL):
                    term = inner[m * 128 : m * 128 + 128, par * 128 : par * 128 + 128].reshape(8, 16, 128)
                    total = total + own_part(m, par * PAIRS + 8 * g, 8) * term
                ens[pl.ds(par * PAIRS + 8 * g, 8)] = total

            def edge(pair, shifts, at):
                wide = []
                for m in range(LOCAL):
                    wide.append(
                        jnp.concatenate([u[m, 32 + 16 * (pair + d) : 48 + 16 * (pair + d), :] for d in shifts], axis=1)
                    )
                inner = jnp.dot(
                    jnp.concatenate(wide, axis=0), amat[at : at + 768, :], preferred_element_type=F32
                )
                for par in range(2):
                    total = jnp.zeros((1, 16, 128), F32)
                    for m in range(LOCAL):
                        term = inner[m * 16 : m * 16 + 16, par * 128 : par * 128 + 128].reshape(1, 16, 128)
                        total = total + own_part(m, par * PAIRS + pair, 1) * term
                    ens[par * PAIRS + pair : par * PAIRS + pair + 1] = total

            @pl.when(g == 0)
            def _():
                edge(0, range(0, 3), 1280)

            @pl.when(g == 3)
            def _():
                edge(PAIRS - 1, range(-2, 1), 2048)

            even = ens[pl.ds(8 * g, 8)]
            odd = ens[pl.ds(PAIRS + 8 * g, 8)]
            both = jnp.stack([even, odd], axis=1).reshape(QUARTER, 16, 128).astype(BF16)
            es[it, pl.ds(g * QUARTER, QUARTER)] = both

            @pl.when(turn_at < 3)
            def _():
                rs_copy(it, k).start()

            @pl.when(turn_at == 3)
            def _():
                rs[it, mm] = both

            return carry

        lax.fori_loop(0, MEMS, group, 0)

    def rs_copy(it, k):
        to = lax.rem(mm + k, MEMS)
        return pltpu.make_async_remote_copy(
            src_ref=es.at[it, pl.ds(to * QUARTER, QUARTER)],
            dst_ref=rs.at[it, mm],
            send_sem=b_send.at[it],
            recv_sem=b_recv.at[it],
            device_id=at_mem(to),
            device_id_type=MESH,
        )

    def wait_rs(it):
        wait_bytes(rs.at[it, 0 : MEMS - 1], b_recv.at[it])
        wait_bytes(rs.at[it, 0 : MEMS - 1], b_send.at[it])
        total = rs[it, 0].astype(F32)
        for m in range(1, MEMS):
            total = total + rs[it, m].astype(F32)
        zs[it] = total.astype(BF16)

    def back_copy(it, tt, m):
        return pltpu.make_async_remote_copy(
            src_ref=zs.at[it, tt],
            dst_ref=back.at[it, me],
            send_sem=c_send.at[it],
            recv_sem=c_recv.at[it],
            device_id={"tile": mm * QUARTER + tt, "mem": m},
            device_id_type=MESH,
        )

    def start_back(it):
        def go(k, carry):
            m = lax.rem(mm + lax.div(k, QUARTER), MEMS)
            tt = lax.rem(me + k, QUARTER)
            itself = jnp.logical_and(mm * QUARTER + tt == me, m == mm)

            @pl.when(jnp.logical_not(itself))
            def _():
                back_copy(it, tt, m).start()

            @pl.when(itself)
            def _():
                pltpu.make_async_copy(zs.at[it, tt], back.at[it, me], c_recv.at[it]).start()

            return carry

        lax.fori_loop(0, TILES, go, 0)

    def wait_back(it):
        wait_bytes(back.at[it], c_recv.at[it])
        to_self = lax.div(me, QUARTER) == mm

        @pl.when(to_self)
        def _():
            wait_bytes(back.at[it, 0 : TILES - 1], c_send.at[it])

        @pl.when(jnp.logical_not(to_self))
        def _():
            wait_bytes(back.at[it], c_send.at[it])

    def gather_back(it):
        wide = jnp.concatenate([back[it, 16 * q : 16 * q + 16].reshape(256, 128) for q in range(4)], axis=1)
        for s in range(STENCIL):
            hs[s] = lax.dot_general(
                onehot[s * 512 : s * 512 + 512, :], wide, (((1,), (1,)), ((), ())), preferred_element_type=F32
            ).astype(BF16)

    def prolong(piece):
        total = None
        for s in range(STENCIL):
            term = lax.dot_general(
                hs[s],
                wv[s, piece * 256 : piece * 256 + 256, :],
                (((1,), (1,)), ((), ())),
                preferred_element_type=F32,
            )
            total = term if total is None else total + term
        return total

    for r in range(4):
        loads[r].wait()
        fill_blocks(r, bv[r].astype(BF16))
    loads[4].wait()
    restrict(0)
    build()
    pl.semaphore_wait(barrier, TILES - 1 + MEMS - 1)
    start_c(0)
    for r in range(4):
        loads[5 + r].wait()
    square = jnp.zeros((1, 128), F32)
    diag = jnp.zeros((1, 128), F32)
    for r in range(4):
        v = bv[r]
        square = square + pack_row(v * v)
        diag = diag + pack_row(v * v * (1.0 + sv[r]))
    sum_start(0, 0, stack_rows([square, diag]))
    loads[9].wait()
    lax.fori_loop(0, LOCAL, turn, 0)
    sum_start(0, 1, sum_end(0, 0))
    first_sums = sum_end(0, 1)
    wait_halo()
    wait_c(0)
    ensemble(0)

    def col_dot(c_it):
        return pack_row(ens[...] * recv_c[c_it, :, 0:16, :].astype(F32))

    sum_start(1, 0, stack_rows([col_dot(0)]))
    wait_rs(0)
    start_back(0)
    sum_start(1, 1, sum_end(1, 0))
    sum_start(1, 2, sum_end(1, 1))
    second_sums = sum_end(1, 2)
    rr = pick(first_sums, 0)
    dad = pick(first_sums, 1) + pick(second_sums, 0)
    alpha = rr / dad
    wait_back(0)
    gather_back(0)
    square = jnp.zeros((1, 128), F32)
    diag = jnp.zeros((1, 128), F32)
    cross = jnp.zeros((1, 128), F32)
    for piece in range(4):
        rr_, half = piece // 2, piece % 2
        total = prolong(piece)
        for p in range(2):
            for q in range(4):
                r = 2 * p + rr_
                cols = slice(q * 512 + half * 256, q * 512 + half * 256 + 256)
                j = 4 * p + q
                d = bv[r, :, cols]
                factor = 1.0 + sv[r, :, cols]
                image = d * factor + total[j * 64 : j * 64 + 64, :]
                ab[r, :, cols] = image
                rnew = d - alpha * image
                fb[j, :, piece * 256 : piece * 256 + 256] = rnew.astype(BF16)
                square = square + pack_row(rnew * rnew)
                diag = diag + pack_row(rnew * rnew * factor)
                cross = cross + pack_row(d * rnew * factor)
    restrict(1)
    start_c(1)
    sum_start(2, 0, stack_rows([square, diag, cross]))
    sum_start(2, 1, sum_end(2, 0))
    third_sums = sum_end(2, 1)
    wait_c(1)
    ensemble(1)
    sum_start(3, 0, stack_rows([col_dot(1), col_dot(0)]))
    wait_rs(1)
    start_back(1)
    sum_start(3, 1, sum_end(3, 0))
    sum_start(3, 2, sum_end(3, 1))
    fourth_sums = sum_end(3, 2)
    new = pick(third_sums, 0)
    beta = new / rr
    both = pick(third_sums, 2) + pick(fourth_sums, 1)
    dad2 = pick(third_sums, 1) + pick(fourth_sums, 0) + 2.0 * beta * both + beta * beta * dad
    alpha2 = new / dad2
    wait_back(1)
    gather_back(1)
    stores = []
    for piece in range(4):
        rr_, half = piece // 2, piece % 2
        total = prolong(piece)
        for p in range(2):
            for q in range(4):
                r = 2 * p + rr_
                cols = slice(q * 512 + half * 256, q * 512 + half * 256 + 256)
                j = 4 * p + q
                d = bv[r, :, cols]
                image = ab[r, :, cols]
                rnew = d - alpha * image
                second = rnew * (1.0 + sv[r, :, cols]) + total[j * 64 : j * 64 + 64, :] + beta * image
                outv[0, r, :, cols] = alpha * d + alpha2 * (rnew + beta * d)
                outv[1, r, :, cols] = rnew - alpha2 * second
        if half == 1:
            for r in (rr_, 2 + rr_):
                stores.append(pltpu.make_async_copy(outv.at[0, r], sol_hbm.at[:, r, :], out_sem.at[r]))
                stores.append(pltpu.make_async_copy(outv.at[1, r], res_hbm.at[:, r, :], out_sem.at[4 + r]))
                stores[-2].start()
                stores[-1].start()
    for store in stores:
        store.wait()


def on_device(right_side, static_var, members, vertical_root, stencil, weights):
    coef = np.repeat(row_blocks().reshape(44, 4), LEV, axis=1)
    coef = jnp.asarray(np.concatenate([coef, np.zeros((4, 256))]), F32)
    order = np.zeros((ROWS, ROWS))
    for i in range(2):
        for par in range(2):
            for pair in range(PAIRS):
                order[i * 64 + par * PAIRS + pair, 4 * pair + 2 * par + i] = 1.0
    perm = jnp.asarray(order, BF16)
    xop = jnp.asarray(column_operator(), BF16)
    vmem = pl.BlockSpec(memory_space=pltpu.VMEM)
    anyspec = pl.BlockSpec(memory_space=pl.ANY)
    field = jax.ShapeDtypeStruct(right_side.shape, F32)
    return pl.pallas_call(
        kernel,
        out_shape=(field, field),
        in_specs=[anyspec] * 3 + [vmem] * 4 + [pl.BlockSpec(memory_space=pltpu.SMEM), anyspec],
        out_specs=(anyspec, anyspec),
        scratch_shapes=[
            pltpu.VMEM((4, LEV, 2048), F32),
            pltpu.VMEM((4, LEV, 2048), F32),
            pltpu.VMEM((4, LEV, 2048), F32),
            pltpu.VMEM((LOCAL, LEV, WIDTH, 128), BF16),
            pltpu.VMEM((COLS, 128), F32),
            pltpu.VMEM((COLS, 128), F32),
            pltpu.VMEM((2, LOCAL, PAIRS, 16, 128), BF16),
            pltpu.VMEM((2, LOCAL, PAIRS, 16, 128), BF16),
            pltpu.VMEM((LOCAL, TILES, 32, 128), BF16),
            pltpu.VMEM((11 * 256, 256), BF16),
            pltpu.VMEM((STENCIL, 1024, 256), BF16),
            pltpu.VMEM((8, LEV, 1024), BF16),
            pltpu.VMEM((2048, 512), BF16),
            pltpu.VMEM((2, TILES, 32, 128), BF16),
            pltpu.VMEM((2, TILES, 32, 128), BF16),
            pltpu.VMEM((COLS, 128), F32),
            pltpu.VMEM((LOCAL, 576, 256), BF16),
            pltpu.VMEM((TILES, 16, 128), F32),
            pltpu.VMEM((2, TILES, 16, 128), BF16),
            pltpu.VMEM((2, MEMS, QUARTER, 16, 128), BF16),
            pltpu.VMEM((2, QUARTER, 16, 128), BF16),
            pltpu.VMEM((2, TILES, 16, 128), BF16),
            pltpu.VMEM((STENCIL, 512, 256), BF16),
            pltpu.VMEM((2, 4, LEV, 2048), F32),
            pltpu.VMEM((4, 3, 8, 128), F32),
            pltpu.VMEM((4, 8, 8, 128), F32),
            pltpu.VMEM((4, 8, 8, 128), F32),
            pltpu.VMEM((4, MEMS, 8, 128), F32),
            pltpu.SemaphoreType.DMA((12,)),
            pltpu.SemaphoreType.DMA((2,)),
            pltpu.SemaphoreType.DMA((2,)),
            pltpu.SemaphoreType.DMA((2,)),
            pltpu.SemaphoreType.DMA((2,)),
            pltpu.SemaphoreType.DMA((2,)),
            pltpu.SemaphoreType.DMA((2,)),
            pltpu.SemaphoreType.DMA((4, 3)),
            pltpu.SemaphoreType.DMA((4, 3)),
            pltpu.SemaphoreType.DMA((2,)),
            pltpu.SemaphoreType.DMA((2,)),
            pltpu.SemaphoreType.DMA((8,)),
        ],
        compiler_params=pltpu.CompilerParams(
            collective_id=0, has_side_effects=True, vmem_limit_bytes=58 * 1024 * 1024
        ),
        name="conjugate_gradient",
    )(right_side, static_var, members, vertical_root, coef, xop, perm, stencil, weights)


def solution(mesh):
    in_specs = (
        P(None, "tile", None),
        P(None, "tile", None),
        P("mem", None, "tile", None),
        P(),
        P("tile", None),
        P(),
    )
    out_specs = (P(None, "tile", None), P(None, "tile", None))
    return jax.shard_map(on_device, mesh=mesh, in_specs=in_specs, out_specs=out_specs, check_vma=False)
```

```python
import functools
import math

import jax
import jax.numpy as jnp
import numpy as np
from jax import lax
from jax.experimental import pallas as pl
from jax.experimental.pallas import tpu as pltpu
from jax.sharding import PartitionSpec as P

LEV = 64
COLS = 1024
BLOCK = 256
STENCIL = 4
REACH = 4
MEMBERS = 20
ROWS = 128
TILES = 64
MEMS = 4
LOCAL = 5
WIDTH = 16
QUARTER = TILES // MEMS
PAIRS = 32
MESH = pl.DeviceIdType.MESH
F32 = jnp.float32
BF16 = jnp.bfloat16


def kernel_taps(reach):
    values = [math.exp(-(offset * offset) / (reach * reach)) for offset in range(-reach, reach + 1)]
    summed = sum(values)
    return np.array([factor / summed for factor in values])


def row_operator():
    taps = kernel_taps(REACH)
    once = np.zeros((ROWS, ROWS))
    for row in range(ROWS):
        for offset in range(-REACH, REACH + 1):
            if 0 <= row + offset < ROWS:
                once[row, row + offset] = taps[offset + REACH]
    return once @ once


def row_blocks():
    twice = row_operator()
    kinds = []
    for group, shifts in ((8, range(-2, 3)), (0, range(0, 3)), (31, range(-2, 1))):
        for shift in shifts:
            at = 4 * (group + shift)
            kinds.append(twice[4 * group : 4 * group + 4, at : at + 4].T)
    return np.stack(kinds)


def column_operator():
    taps = kernel_taps(REACH)
    twice = np.convolve(taps, taps)
    places = list(range(WIDTH)) + list(range(-8, 0)) + list(range(WIDTH, WIDTH + 8))
    out = np.zeros((WIDTH, 2 * WIDTH))
    for to in range(WIDTH):
        for at, place in enumerate(places):
            if abs(place - to) <= 2 * REACH:
                out[to, at] = twice[place - to + 2 * REACH]
    return np.kron(np.eye(8), out)


def kernel(
    b_hbm, s_hbm, mem_hbm, root_ref, coef_ref, xop, perm, st_ref, w_hbm, sol_hbm, res_hbm,
    bv, sv, ab, mraw, wide_t, wide_g, halo_send, halo_recv, mem, amat, wv, fb, onehot, send_c, recv_c, own_c, u, ens, es, rs, zs, back, hs, outv,
    part, sc1, sc2, sc3,
    load_sem, a_send, a_recv, b_send, b_recv, c_send, c_recv, s_send, s_recv, h_send, h_recv, ready, out_sem,
):
    me = lax.axis_index("tile")
    mm = lax.axis_index("mem")

    def wait_bytes(ref, sem):
        pltpu.make_async_copy(ref, ref, sem).wait()

    def at_tile(t):
        return {"tile": t, "mem": mm}

    def at_mem(m):
        return {"tile": me, "mem": m}

    barrier = pltpu.get_barrier_semaphore()

    def greet(k, carry):
        pl.semaphore_signal(barrier, inc=1, device_id=at_tile(lax.rem(me + k, TILES)), device_id_type=MESH)
        return carry

    lax.fori_loop(1, TILES, greet, 0)
    for k in range(1, MEMS):
        pl.semaphore_signal(barrier, inc=1, device_id=at_mem(lax.rem(mm + k, MEMS)), device_id_type=MESH)

    loads = []
    for r in range(4):
        loads.append(pltpu.make_async_copy(b_hbm.at[:, r, :], bv.at[r], load_sem.at[r]))
    loads.append(pltpu.make_async_copy(w_hbm, wv, load_sem.at[4]))
    for r in range(4):
        loads.append(pltpu.make_async_copy(s_hbm.at[:, r, :], sv.at[r], load_sem.at[5 + r]))
    loads.append(pltpu.make_async_copy(mem_hbm, mraw, load_sem.at[9]))
    loads[9].start()
    for load in loads[:9]:
        load.start()

    def build():
        rows_at = lax.broadcasted_iota(jnp.int32, (LEV, 2 * LEV), 0)
        lanes_at = lax.broadcasted_iota(jnp.int32, (LEV, 2 * LEV), 1)
        eye0 = (lanes_at == rows_at).astype(F32)
        eye1 = (lanes_at == rows_at + LEV).astype(F32)
        for s in range(STENCIL):
            for q in range(4):
                e0 = st_ref[q, s]
                e1 = st_ref[4 + q, s]

                def place(j, carry, s=s, q=q, e0=e0, e1=e1):
                    h0 = jnp.where(e0 == j, 1.0, 0.0).astype(F32)
                    h1 = jnp.where(e1 == j, 1.0, 0.0).astype(F32)
                    onehot[pl.ds(pl.multiple_of((s * 8 + j) * LEV, LEV), LEV), q * 128 : q * 128 + 128] = (
                        eye0 * h0 + eye1 * h1
                    ).astype(BF16)
                    return carry

                lax.fori_loop(0, 8, place, 0)
        for m in range(LOCAL):
            u[m, 0:32, :] = jnp.zeros((32, 256), BF16)
            u[m, 544:576, :] = jnp.zeros((32, 256), BF16)
        both = lax.dot_general(
            root_ref[...],
            root_ref[...],
            (((1,), (1,)), ((), ())),
            preferred_element_type=F32,
            precision=lax.Precision.HIGHEST,
        ) * (1.0 / (MEMBERS - 1))
        four = jnp.concatenate([both] * 4, axis=1)

        def scale(n, carry):
            amat[pl.ds(pl.multiple_of(n * LEV, LEV), LEV), :] = (four * coef_ref[pl.ds(n, 1), :]).astype(BF16)
            return carry

        lax.fori_loop(0, 44, scale, 0)

    def halo_copy(side, m):
        to = lax.rem(me + (TILES - 1 if side == 0 else 1), TILES)
        return pltpu.make_async_remote_copy(
            src_ref=halo_send.at[side, m],
            dst_ref=halo_recv.at[side, m],
            send_sem=h_send.at[side],
            recv_sem=h_recv.at[side],
            device_id=at_tile(to),
            device_id_type=MESH,
        )

    def turn(m, carry):
        wide_t[...] = mraw[m].reshape(COLS, 128).astype(F32)
        for c in range(WIDTH):
            at = wide_t[pl.ds(c, LEV, stride=WIDTH), :].astype(BF16)
            rows = lax.dot_general(perm[...], at, (((1,), (1,)), ((), ())), preferred_element_type=F32)
            wide_g[pl.ds(c, TILES, stride=WIDTH), :] = jnp.concatenate([rows[:64], rows[64:]], axis=1)
        turned = wide_g[...]
        mem[m, :, 0:16, :] = turned.reshape(TILES, 16, 128).astype(BF16)
        halves = turned.reshape(TILES, 2, 8, 128)
        for side in range(2):
            halo_send[side, m] = halves[:, side].reshape(PAIRS, 16, 128).astype(BF16)
        return carry

    def wait_halo():
        for side in range(2):
            wait_bytes(halo_recv.at[side], h_recv.at[side])
            wait_bytes(halo_send.at[side], h_send.at[side])

        def join(m, carry):
            before = halo_recv[1, m].astype(F32).reshape(TILES, 8, 128)
            after = halo_recv[0, m].astype(F32).reshape(TILES, 8, 128)
            mem[m, :, 16:32, :] = jnp.concatenate([before, after], axis=1).astype(BF16)
            return carry

        lax.fori_loop(0, LOCAL, join, 0)

    def pack_row(v):
        return jnp.sum(v.reshape(-1, 8, 128), axis=0).sum(axis=0, keepdims=True)

    def restrict(it):
        acc = None
        for s in range(STENCIL):
            rows = []
            for q in range(4):
                for i in range(2):
                    rows.append(fb[st_ref[4 * i + q, s]])
            term = jnp.dot(jnp.concatenate(rows, axis=0), wv[s], preferred_element_type=F32)
            acc = term if acc is None else acc + term
        for q in range(4):
            turned = acc[q * 128 : q * 128 + 128].T
            own_c[q * 256 : q * 256 + 256, :] = turned
        grid = own_c[...].reshape(TILES, 2, 8, 128)
        first, last = grid[:, 0], grid[:, 1]
        before = jnp.concatenate([last[TILES - 1 :], last[: TILES - 1]], axis=0)
        after = jnp.concatenate([first[1:], first[:1]], axis=0)
        send_c[it, :, 0:16, :] = jnp.concatenate([first, last], axis=1).astype(BF16)
        send_c[it, :, 16:32, :] = jnp.concatenate([before, after], axis=1).astype(BF16)

    def fill_blocks(r, field):
        p, rr = r // 2, r % 2
        for q in range(4):
            fb[4 * p + q, :, rr * 512 : rr * 512 + 512] = field[:, q * 512 : q * 512 + 512]

    group_of_me = lax.div(me, QUARTER)
    mine = lax.rem(me, 2) * PAIRS + lax.div(me, 2)


    def c_copy(it, t):
        return pltpu.make_async_remote_copy(
            src_ref=send_c.at[it, t],
            dst_ref=recv_c.at[it, mine],
            send_sem=a_send.at[it],
            recv_sem=a_recv.at[it, group_of_me],
            device_id=at_tile(t),
            device_id_type=MESH,
        )

    def start_c(it):
        def go(k, carry):
            c_copy(it, lax.rem(me + k, TILES)).start()
            return carry

        lax.fori_loop(1, TILES, go, 0)
        pltpu.make_async_copy(send_c.at[it, me], recv_c.at[it, mine], a_recv.at[it, group_of_me]).start()

    def wait_c(it):
        wait_bytes(send_c.at[it, 0 : TILES - 1], a_send.at[it])

    low = lax.rem(me, 8)
    high = lax.div(me, 8)

    def sum_copy(x, stage, k):
        if stage == 0:
            slot, dst = low, sc1
            to = at_tile(high * 8 + lax.rem(low + k, 8))
        elif stage == 1:
            slot, dst = high, sc2
            to = at_tile(lax.rem(high + k, 8) * 8 + low)
        else:
            slot, dst = mm, sc3
            to = at_mem(lax.rem(mm + k, MEMS))
        return pltpu.make_async_remote_copy(
            src_ref=part.at[x, stage],
            dst_ref=dst.at[x, slot],
            send_sem=s_send.at[x, stage],
            recv_sem=s_recv.at[x, stage],
            device_id=to,
            device_id_type=MESH,
        )

    def sum_start(x, stage, value):
        part[x, stage] = value
        if stage == 0:
            sc1[x, low] = value
        elif stage == 1:
            sc2[x, high] = value
        else:
            sc3[x, mm] = value

        def go(k, carry):
            sum_copy(x, stage, k).start()
            return carry

        lax.fori_loop(1, MEMS if stage == 2 else 8, go, 0)

    def sum_end(x, stage):
        held = (sc1, sc2, sc3)[stage]
        count = MEMS - 1 if stage == 2 else 7
        wait_bytes(held.at[x, 0:count], s_recv.at[x, stage])
        wait_bytes(held.at[x, 0:count], s_send.at[x, stage])
        return jnp.sum(held[x], axis=0)

    def stack_rows(rows):
        rows = rows + [jnp.zeros((8 - len(rows), 128), F32)]
        return jnp.concatenate(rows, axis=0)

    def pick(tile, row):
        return jnp.sum(tile[row : row + 1, :], axis=1, keepdims=True)

    def mix(it):
        def group(turn_at, carry):
            g = lax.rem(group_of_me + 3 - turn_at, 4)
            wait_bytes(recv_c.at[it, 0:QUARTER], a_recv.at[it, g])
            for m in range(LOCAL):
                lanes = []
                for par in range(2):
                    at = par * PAIRS + 8 * g
                    lanes.append((mem[m, pl.ds(at, 8)] * recv_c[it, pl.ds(at, 8)]).reshape(256, 128))
                mixed = jnp.dot(xop[...], jnp.concatenate(lanes, axis=1), preferred_element_type=F32)
                u[m, pl.ds(pl.multiple_of(32 + 128 * g, 32), 128), :] = mixed.astype(BF16)
            return carry

        lax.fori_loop(0, 4, group, 0)

    def own_part(m, at, count):
        return mem[m, pl.ds(at, count), 0:16, :].astype(F32)

    to_self = lax.rem(group_of_me + me, MEMS) == mm
    segment = lax.rem(mm + TILES - me, MEMS)
    slot = lax.rem(me, QUARTER)

    def out_go(it, t):
        itself = jnp.logical_and(t == me, to_self)

        @pl.when(jnp.logical_not(itself))
        def _():
            pltpu.make_async_remote_copy(
                src_ref=es.at[it, t],
                dst_ref=rs.at[it, mm, slot],
                send_sem=b_send.at[it],
                recv_sem=b_recv.at[it],
                device_id={"tile": t, "mem": lax.rem(group_of_me + t, MEMS)},
                device_id_type=MESH,
            ).start()

        @pl.when(itself)
        def _():
            pltpu.make_async_copy(es.at[it, t], rs.at[it, mm, slot], b_recv.at[it]).start()

    def ensemble(it):
        mix(it)

        def group(turn_at, carry):
            g = lax.rem(me + mm + turn_at, 4)
            wide = []
            for m in range(LOCAL):
                pieces = []
                for d in range(-2, 3):
                    pieces.append(u[m, pl.ds(pl.multiple_of(32 + 128 * g + 16 * d, 16), 128), :])
                wide.append(jnp.concatenate(pieces, axis=1))
            inner = jnp.dot(jnp.concatenate(wide, axis=0), amat[0:1280, :], preferred_element_type=F32)
            for par in range(2):
                total = jnp.zeros((8, 16, 128), F32)
                for m in range(LOCAL):
                    term = inner[m * 128 : m * 128 + 128, par * 128 : par * 128 + 128].reshape(8, 16, 128)
                    total = total + own_part(m, par * PAIRS + 8 * g, 8) * term
                ens[pl.ds(par * PAIRS + 8 * g, 8)] = total

            def edge(pair, shifts, at):
                wide = []
                for m in range(LOCAL):
                    wide.append(
                        jnp.concatenate([u[m, 32 + 16 * (pair + d) : 48 + 16 * (pair + d), :] for d in shifts], axis=1)
                    )
                inner = jnp.dot(
                    jnp.concatenate(wide, axis=0), amat[at : at + 768, :], preferred_element_type=F32
                )
                for par in range(2):
                    total = jnp.zeros((1, 16, 128), F32)
                    for m in range(LOCAL):
                        term = inner[m * 16 : m * 16 + 16, par * 128 : par * 128 + 128].reshape(1, 16, 128)
                        total = total + own_part(m, par * PAIRS + pair, 1) * term
                    ens[par * PAIRS + pair : par * PAIRS + pair + 1] = total

            @pl.when(g == 0)
            def _():
                edge(0, range(0, 3), 1280)

            @pl.when(g == 3)
            def _():
                edge(PAIRS - 1, range(-2, 1), 2048)

            even = ens[pl.ds(8 * g, 8)]
            odd = ens[pl.ds(PAIRS + 8 * g, 8)]
            both = jnp.stack([even, odd], axis=1).reshape(QUARTER, 16, 128).astype(BF16)
            es[it, pl.ds(g * QUARTER, QUARTER)] = both

            def go(k, inner_carry):
                out_go(it, g * QUARTER + lax.rem(me + k, QUARTER))
                return inner_carry

            lax.fori_loop(0, QUARTER, go, 0)
            return carry

        lax.fori_loop(0, MEMS, group, 0)

    def wait_rs(it):
        wait_bytes(es.at[it], b_recv.at[it])

        @pl.when(to_self)
        def _():
            wait_bytes(es.at[it, 0 : TILES - 1], b_send.at[it])

        @pl.when(jnp.logical_not(to_self))
        def _():
            wait_bytes(es.at[it], b_send.at[it])

        total = rs[it, 0].astype(F32)
        for m in range(1, MEMS):
            total = total + rs[it, m].astype(F32)
        zs[it] = total.astype(BF16)

    def back_copy(it, k):
        return pltpu.make_async_remote_copy(
            src_ref=zs.at[it],
            dst_ref=back.at[it, pl.ds(segment * QUARTER, QUARTER)],
            send_sem=c_send.at[it],
            recv_sem=c_recv.at[it],
            device_id=at_mem(lax.rem(mm + k, MEMS)),
            device_id_type=MESH,
        )

    def start_back(it):
        for k in (2, 1, 3):
            back_copy(it, k).start()
        back[it, pl.ds(segment * QUARTER, QUARTER)] = zs[it]

    def wait_back(it):
        wait_bytes(back.at[it, 0 : 3 * QUARTER], c_recv.at[it])
        wait_bytes(back.at[it, 0 : 3 * QUARTER], c_send.at[it])

    def gather_back(it):
        wide = jnp.concatenate([back[it, 16 * q : 16 * q + 16].reshape(256, 128) for q in range(4)], axis=1)
        for s in range(STENCIL):
            hs[s] = lax.dot_general(
                onehot[s * 512 : s * 512 + 512, :], wide, (((1,), (1,)), ((), ())), preferred_element_type=F32
            ).astype(BF16)

    def prolong(piece):
        total = None
        for s in range(STENCIL):
            term = lax.dot_general(
                hs[s],
                wv[s, piece * 256 : piece * 256 + 256, :],
                (((1,), (1,)), ((), ())),
                preferred_element_type=F32,
            )
            total = term if total is None else total + term
        return total

    loads[9].wait()
    lax.fori_loop(0, LOCAL, turn, 0)
    pl.semaphore_wait(barrier, TILES - 1 + MEMS - 1)

    def send_halo(m, carry):
        halo_copy(0, m).start()
        halo_copy(1, m).start()
        return carry

    lax.fori_loop(0, LOCAL, send_halo, 0)
    for k in range(1, MEMS):
        pl.semaphore_signal(ready, inc=1, device_id=at_mem(lax.rem(mm + k, MEMS)), device_id_type=MESH)
    for r in range(4):
        loads[r].wait()
        fill_blocks(r, bv[r].astype(BF16))
    loads[4].wait()
    restrict(0)
    start_c(0)
    for r in range(4):
        loads[5 + r].wait()
    square = jnp.zeros((1, 128), F32)
    diag = jnp.zeros((1, 128), F32)
    for r in range(4):
        v = bv[r]
        square = square + pack_row(v * v)
        diag = diag + pack_row(v * v * (1.0 + sv[r]))
    sum_start(0, 0, stack_rows([square, diag]))
    build()
    wait_halo()
    sum_start(0, 1, sum_end(0, 0))
    pl.semaphore_wait(ready, MEMS - 1)
    ensemble(0)

    def col_dot(c_it):
        return pack_row(ens[...] * recv_c[c_it, :, 0:16, :].astype(F32))

    sum_start(1, 0, stack_rows([col_dot(0)]))
    wait_c(0)
    first_sums = sum_end(0, 1)
    sum_start(1, 1, sum_end(1, 0))
    wait_rs(0)
    sum_start(1, 2, sum_end(1, 1))
    start_back(0)
    second_sums = sum_end(1, 2)
    rr = pick(first_sums, 0)
    dad = pick(first_sums, 1) + pick(second_sums, 0)
    alpha = rr / dad
    wait_back(0)
    gather_back(0)
    square = jnp.zeros((1, 128), F32)
    diag = jnp.zeros((1, 128), F32)
    cross = jnp.zeros((1, 128), F32)
    for piece in range(4):
        rr_, half = piece // 2, piece % 2
        total = prolong(piece)
        for p in range(2):
            for q in range(4):
                r = 2 * p + rr_
                cols = slice(q * 512 + half * 256, q * 512 + half * 256 + 256)
                j = 4 * p + q
                d = bv[r, :, cols]
                factor = 1.0 + sv[r, :, cols]
                image = d * factor + total[j * 64 : j * 64 + 64, :]
                ab[r, :, cols] = image
                rnew = d - alpha * image
                fb[j, :, piece * 256 : piece * 256 + 256] = rnew.astype(BF16)
                square = square + pack_row(rnew * rnew)
                diag = diag + pack_row(rnew * rnew * factor)
                cross = cross + pack_row(d * rnew * factor)
    sum_start(2, 0, stack_rows([square, diag, cross]))
    restrict(1)
    sum_start(2, 1, sum_end(2, 0))
    start_c(1)
    ensemble(1)
    sum_start(3, 0, stack_rows([col_dot(1), col_dot(0)]))
    wait_c(1)
    third_sums = sum_end(2, 1)
    sum_start(3, 1, sum_end(3, 0))
    wait_rs(1)
    sum_start(3, 2, sum_end(3, 1))
    start_back(1)
    fourth_sums = sum_end(3, 2)
    new = pick(third_sums, 0)
    beta = new / rr
    both = pick(third_sums, 2) + pick(fourth_sums, 1)
    dad2 = pick(third_sums, 1) + pick(fourth_sums, 0) + 2.0 * beta * both + beta * beta * dad
    alpha2 = new / dad2
    wait_back(1)
    gather_back(1)
    stores = []
    for piece in range(4):
        rr_, half = piece // 2, piece % 2
        total = prolong(piece)
        for p in range(2):
            for q in range(4):
                r = 2 * p + rr_
                cols = slice(q * 512 + half * 256, q * 512 + half * 256 + 256)
                j = 4 * p + q
                d = bv[r, :, cols]
                image = ab[r, :, cols]
                rnew = d - alpha * image
                second = rnew * (1.0 + sv[r, :, cols]) + total[j * 64 : j * 64 + 64, :] + beta * image
                outv[0, r, :, cols] = alpha * d + alpha2 * (rnew + beta * d)
                outv[1, r, :, cols] = rnew - alpha2 * second
        if half == 1:
            for r in (rr_, 2 + rr_):
                stores.append(pltpu.make_async_copy(outv.at[0, r], sol_hbm.at[:, r, :], out_sem.at[r]))
                stores.append(pltpu.make_async_copy(outv.at[1, r], res_hbm.at[:, r, :], out_sem.at[4 + r]))
                stores[-2].start()
                stores[-1].start()
    for store in stores:
        store.wait()


def on_device(right_side, static_var, members, vertical_root, stencil, weights):
    coef = np.repeat(row_blocks().reshape(44, 4), LEV, axis=1)
    coef = jnp.asarray(np.concatenate([coef, np.zeros((4, 256))]), F32)
    order = np.zeros((ROWS, ROWS))
    for i in range(2):
        for par in range(2):
            for pair in range(PAIRS):
                order[i * 64 + par * PAIRS + pair, 4 * pair + 2 * par + i] = 1.0
    perm = jnp.asarray(order, BF16)
    xop = jnp.asarray(column_operator(), BF16)
    vmem = pl.BlockSpec(memory_space=pltpu.VMEM)
    anyspec = pl.BlockSpec(memory_space=pl.ANY)
    field = jax.ShapeDtypeStruct(right_side.shape, F32)
    return pl.pallas_call(
        kernel,
        out_shape=(field, field),
        in_specs=[anyspec] * 3 + [vmem] * 4 + [pl.BlockSpec(memory_space=pltpu.SMEM), anyspec],
        out_specs=(anyspec, anyspec),
        scratch_shapes=[
            pltpu.VMEM((4, LEV, 2048), F32),
            pltpu.VMEM((4, LEV, 2048), F32),
            pltpu.VMEM((4, LEV, 2048), F32),
            pltpu.VMEM((LOCAL, LEV, WIDTH, 128), BF16),
            pltpu.VMEM((COLS, 128), F32),
            pltpu.VMEM((COLS, 128), F32),
            pltpu.VMEM((2, LOCAL, PAIRS, 16, 128), BF16),
            pltpu.VMEM((2, LOCAL, PAIRS, 16, 128), BF16),
            pltpu.VMEM((LOCAL, TILES, 32, 128), BF16),
            pltpu.VMEM((11 * 256, 256), BF16),
            pltpu.VMEM((STENCIL, 1024, 256), BF16),
            pltpu.VMEM((8, LEV, 1024), BF16),
            pltpu.VMEM((2048, 512), BF16),
            pltpu.VMEM((2, TILES, 32, 128), BF16),
            pltpu.VMEM((2, TILES, 32, 128), BF16),
            pltpu.VMEM((COLS, 128), F32),
            pltpu.VMEM((LOCAL, 576, 256), BF16),
            pltpu.VMEM((TILES, 16, 128), F32),
            pltpu.VMEM((2, TILES, 16, 128), BF16),
            pltpu.VMEM((2, MEMS, QUARTER, 16, 128), BF16),
            pltpu.VMEM((2, QUARTER, 16, 128), BF16),
            pltpu.VMEM((2, TILES, 16, 128), BF16),
            pltpu.VMEM((STENCIL, 512, 256), BF16),
            pltpu.VMEM((2, 4, LEV, 2048), F32),
            pltpu.VMEM((4, 3, 8, 128), F32),
            pltpu.VMEM((4, 8, 8, 128), F32),
            pltpu.VMEM((4, 8, 8, 128), F32),
            pltpu.VMEM((4, MEMS, 8, 128), F32),
            pltpu.SemaphoreType.DMA((12,)),
            pltpu.SemaphoreType.DMA((2,)),
            pltpu.SemaphoreType.DMA((2, 4)),
            pltpu.SemaphoreType.DMA((2,)),
            pltpu.SemaphoreType.DMA((2,)),
            pltpu.SemaphoreType.DMA((2,)),
            pltpu.SemaphoreType.DMA((2,)),
            pltpu.SemaphoreType.DMA((4, 3)),
            pltpu.SemaphoreType.DMA((4, 3)),
            pltpu.SemaphoreType.DMA((2,)),
            pltpu.SemaphoreType.DMA((2,)),
            pltpu.SemaphoreType.REGULAR,
            pltpu.SemaphoreType.DMA((8,)),
        ],
        compiler_params=pltpu.CompilerParams(
            collective_id=0, has_side_effects=True, vmem_limit_bytes=58 * 1024 * 1024
        ),
        name="conjugate_gradient",
    )(right_side, static_var, members, vertical_root, coef, xop, perm, stencil, weights)


def solution(mesh):
    in_specs = (
        P(None, "tile", None),
        P(None, "tile", None),
        P("mem", None, "tile", None),
        P(),
        P("tile", None),
        P(),
    )
    out_specs = (P(None, "tile", None), P(None, "tile", None))
    return jax.shard_map(on_device, mesh=mesh, in_specs=in_specs, out_specs=out_specs, check_vma=False)
```

```python
import functools
import math

import jax
import jax.numpy as jnp
import numpy as np
from jax import lax
from jax.experimental import pallas as pl
from jax.experimental.pallas import tpu as pltpu
from jax.sharding import PartitionSpec as P

LEV = 64
COLS = 1024
BLOCK = 256
STENCIL = 4
REACH = 4
MEMBERS = 20
ROWS = 128
TILES = 64
MEMS = 4
LOCAL = 5
WIDTH = 16
QUARTER = TILES // MEMS
PAIRS = 32
MESH = pl.DeviceIdType.MESH
F32 = jnp.float32
BF16 = jnp.bfloat16


def kernel_taps(reach):
    values = [math.exp(-(offset * offset) / (reach * reach)) for offset in range(-reach, reach + 1)]
    summed = sum(values)
    return np.array([factor / summed for factor in values])


def row_operator():
    taps = kernel_taps(REACH)
    once = np.zeros((ROWS, ROWS))
    for row in range(ROWS):
        for offset in range(-REACH, REACH + 1):
            if 0 <= row + offset < ROWS:
                once[row, row + offset] = taps[offset + REACH]
    return once @ once


def row_blocks():
    twice = row_operator()
    kinds = []
    for group, shifts in ((8, range(-2, 3)), (0, range(0, 3)), (31, range(-2, 1))):
        for shift in shifts:
            at = 4 * (group + shift)
            kinds.append(twice[4 * group : 4 * group + 4, at : at + 4].T)
    return np.stack(kinds)


def column_operator():
    taps = kernel_taps(REACH)
    twice = np.convolve(taps, taps)
    places = list(range(WIDTH)) + list(range(-8, 0)) + list(range(WIDTH, WIDTH + 8))
    out = np.zeros((WIDTH, 2 * WIDTH))
    for to in range(WIDTH):
        for at, place in enumerate(places):
            if abs(place - to) <= 2 * REACH:
                out[to, at] = twice[place - to + 2 * REACH]
    return np.kron(np.eye(8), out)


def kernel(
    b_hbm, s_hbm, mem_hbm, root_hbm, coef_hbm, xop_hbm, perm_hbm, st_hbm, w_hbm, sol_hbm, res_hbm,
    root_ref, coef_ref, xop, perm, st_ref, bv, sv, ab, mraw, wide_t, wide_g, halo_send, halo_recv, mem, amat, wv, fb, onehot, send_c, recv_c, own_c, u, ens, es, rs, zs, back, hs, outv,
    part, sums,
    load_sem, a_send, a_recv, b_send, b_recv, c_send, c_recv, s_send, s_recv, h_send, h_recv, ready, out_sem,
):
    me = lax.axis_index("tile")
    mm = lax.axis_index("mem")

    def wait_bytes(ref, sem):
        pltpu.make_async_copy(ref, ref, sem).wait()

    def at_tile(t):
        return {"tile": t, "mem": mm}

    def at_mem(m):
        return {"tile": me, "mem": m}

    barrier = pltpu.get_barrier_semaphore()

    def greet(k, carry):
        pl.semaphore_signal(barrier, inc=1, device_id=at_tile(lax.rem(me + k, TILES)), device_id_type=MESH)
        return carry

    lax.fori_loop(1, TILES, greet, 0)
    for k in range(1, MEMS):
        pl.semaphore_signal(barrier, inc=1, device_id=at_mem(lax.rem(mm + k, MEMS)), device_id_type=MESH)

    loads = []
    for r in range(4):
        loads.append(pltpu.make_async_copy(b_hbm.at[:, r, :], bv.at[r], load_sem.at[r]))
    loads.append(pltpu.make_async_copy(w_hbm, wv, load_sem.at[4]))
    for r in range(4):
        loads.append(pltpu.make_async_copy(s_hbm.at[:, r, :], sv.at[r], load_sem.at[5 + r]))
    loads.append(pltpu.make_async_copy(mem_hbm, mraw, load_sem.at[9]))
    loads.append(pltpu.make_async_copy(perm_hbm, perm, load_sem.at[10]))
    loads.append(pltpu.make_async_copy(st_hbm, st_ref, load_sem.at[11]))
    loads.append(pltpu.make_async_copy(root_hbm, root_ref, load_sem.at[12]))
    loads.append(pltpu.make_async_copy(coef_hbm, coef_ref, load_sem.at[13]))
    loads.append(pltpu.make_async_copy(xop_hbm, xop, load_sem.at[14]))
    for load in loads[9:11] + loads[:9] + loads[11:]:
        load.start()

    def build():
        rows_at = lax.broadcasted_iota(jnp.int32, (LEV, 2 * LEV), 0)
        lanes_at = lax.broadcasted_iota(jnp.int32, (LEV, 2 * LEV), 1)
        eye0 = (lanes_at == rows_at).astype(F32)
        eye1 = (lanes_at == rows_at + LEV).astype(F32)
        for s in range(STENCIL):
            for q in range(4):
                e0 = st_ref[s, q]
                e1 = st_ref[s, 4 + q]

                def place(j, carry, s=s, q=q, e0=e0, e1=e1):
                    h0 = jnp.where(e0 == j, 1.0, 0.0).astype(F32)
                    h1 = jnp.where(e1 == j, 1.0, 0.0).astype(F32)
                    onehot[pl.ds(pl.multiple_of((s * 8 + j) * LEV, LEV), LEV), q * 128 : q * 128 + 128] = (
                        eye0 * h0 + eye1 * h1
                    ).astype(BF16)
                    return carry

                lax.fori_loop(0, 8, place, 0)
        for m in range(LOCAL):
            u[m, 0:32, :] = jnp.zeros((32, 256), BF16)
            u[m, 544:576, :] = jnp.zeros((32, 256), BF16)
        both = lax.dot_general(
            root_ref[...],
            root_ref[...],
            (((1,), (1,)), ((), ())),
            preferred_element_type=F32,
            precision=lax.Precision.HIGHEST,
        ) * (1.0 / (MEMBERS - 1))
        four = jnp.concatenate([both] * 4, axis=1)

        def scale(n, carry):
            amat[pl.ds(pl.multiple_of(n * LEV, LEV), LEV), :] = (four * coef_ref[pl.ds(n, 1), :]).astype(BF16)
            return carry

        lax.fori_loop(0, 44, scale, 0)

    def halo_copy(side, m):
        to = lax.rem(me + (TILES - 1 if side == 0 else 1), TILES)
        return pltpu.make_async_remote_copy(
            src_ref=halo_send.at[side, m],
            dst_ref=halo_recv.at[side, m],
            send_sem=h_send.at[side],
            recv_sem=h_recv.at[side],
            device_id=at_tile(to),
            device_id_type=MESH,
        )

    def turn(m, carry):
        wide_t[...] = mraw[m].reshape(COLS, 128).astype(F32)
        for c in range(WIDTH):
            at = wide_t[pl.ds(c, LEV, stride=WIDTH), :].astype(BF16)
            rows = lax.dot_general(perm[...], at, (((1,), (1,)), ((), ())), preferred_element_type=F32)
            wide_g[pl.ds(c, TILES, stride=WIDTH), :] = jnp.concatenate([rows[:64], rows[64:]], axis=1)
        turned = wide_g[...]
        mem[m, :, 0:16, :] = turned.reshape(TILES, 16, 128).astype(BF16)
        halves = turned.reshape(TILES, 2, 8, 128)
        for side in range(2):
            halo_send[side, m] = halves[:, side].reshape(PAIRS, 16, 128).astype(BF16)
        return carry

    def wait_halo():
        for side in range(2):
            wait_bytes(halo_recv.at[side], h_recv.at[side])
            wait_bytes(halo_send.at[side], h_send.at[side])

        def join(m, carry):
            before = halo_recv[1, m].astype(F32).reshape(TILES, 8, 128)
            after = halo_recv[0, m].astype(F32).reshape(TILES, 8, 128)
            mem[m, :, 16:32, :] = jnp.concatenate([before, after], axis=1).astype(BF16)
            return carry

        lax.fori_loop(0, LOCAL, join, 0)

    def pack_row(v):
        return jnp.sum(v.reshape(-1, 8, 128), axis=0).sum(axis=0, keepdims=True)

    def restrict(it):
        acc = None
        for s in range(STENCIL):
            rows = []
            for q in range(4):
                for i in range(2):
                    rows.append(fb[st_ref[s, 4 * i + q]])
            term = jnp.dot(jnp.concatenate(rows, axis=0), wv[s], preferred_element_type=F32)
            acc = term if acc is None else acc + term
        for q in range(4):
            turned = acc[q * 128 : q * 128 + 128].T
            own_c[q * 256 : q * 256 + 256, :] = turned
        grid = own_c[...].reshape(TILES, 2, 8, 128)
        first, last = grid[:, 0], grid[:, 1]
        before = jnp.concatenate([last[TILES - 1 :], last[: TILES - 1]], axis=0)
        after = jnp.concatenate([first[1:], first[:1]], axis=0)
        send_c[it, :, 0:16, :] = jnp.concatenate([first, last], axis=1).astype(BF16)
        send_c[it, :, 16:32, :] = jnp.concatenate([before, after], axis=1).astype(BF16)

    def fill_blocks(r, field):
        p, rr = r // 2, r % 2
        for q in range(4):
            fb[4 * p + q, :, rr * 512 : rr * 512 + 512] = field[:, q * 512 : q * 512 + 512]

    group_of_me = lax.div(me, QUARTER)
    mine = lax.rem(me, 2) * PAIRS + lax.div(me, 2)


    def c_copy(it, t):
        return pltpu.make_async_remote_copy(
            src_ref=send_c.at[it, t],
            dst_ref=recv_c.at[it, mine],
            send_sem=a_send.at[it],
            recv_sem=a_recv.at[it, group_of_me],
            device_id=at_tile(t),
            device_id_type=MESH,
        )

    def start_c(it):
        def go(k, carry):
            c_copy(it, lax.rem(me + k, TILES)).start()
            return carry

        lax.fori_loop(1, TILES, go, 0)
        pltpu.make_async_copy(send_c.at[it, me], recv_c.at[it, mine], a_recv.at[it, group_of_me]).start()

    def wait_c(it):
        wait_bytes(send_c.at[it, 0 : TILES - 1], a_send.at[it])

    def sum_peers(x):
        return 16 if x % 2 else 8

    def sum_place(x, stage):
        if x % 2:
            return mm * 4 + lax.rem(me, 4) if stage == 0 else lax.div(me, 4)
        return lax.rem(me, 8) if stage == 0 else lax.div(me, 8)

    def sum_copy(x, stage, k):
        peer = lax.rem(sum_place(x, stage) + k, sum_peers(x))
        if x % 2:
            if stage == 0:
                to = {"tile": lax.div(me, 4) * 4 + lax.rem(peer, 4), "mem": lax.div(peer, 4)}
            else:
                to = at_tile(peer * 4 + lax.rem(me, 4))
        else:
            to = at_tile(lax.div(me, 8) * 8 + peer if stage == 0 else peer * 8 + lax.rem(me, 8))
        return pltpu.make_async_remote_copy(
            src_ref=part.at[x, stage],
            dst_ref=sums.at[x, stage, sum_place(x, stage)],
            send_sem=s_send.at[x, stage],
            recv_sem=s_recv.at[x, stage],
            device_id=to,
            device_id_type=MESH,
        )

    def sum_start(x, stage, value):
        part[x, stage] = value
        sums[x, stage, sum_place(x, stage)] = value

        def go(k, carry):
            sum_copy(x, stage, k).start()
            return carry

        lax.fori_loop(1, sum_peers(x), go, 0)

    def sum_end(x, stage):
        wait_bytes(sums.at[x, stage, 0 : sum_peers(x) - 1], s_recv.at[x, stage])
        wait_bytes(sums.at[x, stage, 0 : sum_peers(x) - 1], s_send.at[x, stage])
        return jnp.sum(sums[x, stage, 0 : sum_peers(x)], axis=0)

    def stack_rows(rows):
        rows = rows + [jnp.zeros((8 - len(rows), 128), F32)]
        return jnp.concatenate(rows, axis=0)

    def pick(tile, row):
        return jnp.sum(tile[row : row + 1, :], axis=1, keepdims=True)

    def mix(it):
        def group(turn_at, carry):
            g = lax.rem(group_of_me + 3 - turn_at, 4)
            wait_bytes(recv_c.at[it, 0:QUARTER], a_recv.at[it, g])
            for m in range(LOCAL):
                lanes = []
                for par in range(2):
                    at = par * PAIRS + 8 * g
                    lanes.append((mem[m, pl.ds(at, 8)] * recv_c[it, pl.ds(at, 8)]).reshape(256, 128))
                mixed = jnp.dot(xop[...], jnp.concatenate(lanes, axis=1), preferred_element_type=F32)
                u[m, pl.ds(pl.multiple_of(32 + 128 * g, 32), 128), :] = mixed.astype(BF16)
            return carry

        lax.fori_loop(0, 4, group, 0)

    def own_part(m, at, count):
        return mem[m, pl.ds(at, count), 0:16, :].astype(F32)

    to_self = lax.rem(group_of_me + me, MEMS) == mm
    segment = lax.rem(mm + TILES - me, MEMS)
    slot = lax.rem(me, QUARTER)

    def out_go(it, t):
        itself = jnp.logical_and(t == me, to_self)

        @pl.when(jnp.logical_not(itself))
        def _():
            pltpu.make_async_remote_copy(
                src_ref=es.at[it, t],
                dst_ref=rs.at[it, mm, slot],
                send_sem=b_send.at[it],
                recv_sem=b_recv.at[it],
                device_id={"tile": t, "mem": lax.rem(group_of_me + t, MEMS)},
                device_id_type=MESH,
            ).start()

        @pl.when(itself)
        def _():
            pltpu.make_async_copy(es.at[it, t], rs.at[it, mm, slot], b_recv.at[it]).start()

    def ensemble(it):
        mix(it)

        def group(turn_at, carry):
            g = lax.rem(me + mm + turn_at, 4)
            wide = []
            for m in range(LOCAL):
                pieces = []
                for d in range(-2, 3):
                    pieces.append(u[m, pl.ds(pl.multiple_of(32 + 128 * g + 16 * d, 16), 128), :])
                wide.append(jnp.concatenate(pieces, axis=1))
            inner = jnp.dot(jnp.concatenate(wide, axis=0), amat[0:1280, :], preferred_element_type=F32)
            for par in range(2):
                total = jnp.zeros((8, 16, 128), F32)
                for m in range(LOCAL):
                    term = inner[m * 128 : m * 128 + 128, par * 128 : par * 128 + 128].reshape(8, 16, 128)
                    total = total + own_part(m, par * PAIRS + 8 * g, 8) * term
                ens[pl.ds(par * PAIRS + 8 * g, 8)] = total

            def edge(pair, shifts, at):
                wide = []
                for m in range(LOCAL):
                    wide.append(
                        jnp.concatenate([u[m, 32 + 16 * (pair + d) : 48 + 16 * (pair + d), :] for d in shifts], axis=1)
                    )
                inner = jnp.dot(
                    jnp.concatenate(wide, axis=0), amat[at : at + 768, :], preferred_element_type=F32
                )
                for par in range(2):
                    total = jnp.zeros((1, 16, 128), F32)
                    for m in range(LOCAL):
                        term = inner[m * 16 : m * 16 + 16, par * 128 : par * 128 + 128].reshape(1, 16, 128)
                        total = total + own_part(m, par * PAIRS + pair, 1) * term
                    ens[par * PAIRS + pair : par * PAIRS + pair + 1] = total

            @pl.when(g == 0)
            def _():
                edge(0, range(0, 3), 1280)

            @pl.when(g == 3)
            def _():
                edge(PAIRS - 1, range(-2, 1), 2048)

            even = ens[pl.ds(8 * g, 8)]
            odd = ens[pl.ds(PAIRS + 8 * g, 8)]
            both = jnp.stack([even, odd], axis=1).reshape(QUARTER, 16, 128).astype(BF16)
            es[it, pl.ds(g * QUARTER, QUARTER)] = both

            def go(k, inner_carry):
                out_go(it, g * QUARTER + lax.rem(me + k, QUARTER))
                return inner_carry

            lax.fori_loop(0, QUARTER, go, 0)
            return carry

        lax.fori_loop(0, MEMS, group, 0)

    def wait_rs(it):
        wait_bytes(es.at[it], b_recv.at[it])

        @pl.when(to_self)
        def _():
            wait_bytes(es.at[it, 0 : TILES - 1], b_send.at[it])

        @pl.when(jnp.logical_not(to_self))
        def _():
            wait_bytes(es.at[it], b_send.at[it])

        total = rs[it, 0].astype(F32)
        for m in range(1, MEMS):
            total = total + rs[it, m].astype(F32)
        zs[it] = total.astype(BF16)

    def back_copy(it, k):
        return pltpu.make_async_remote_copy(
            src_ref=zs.at[it],
            dst_ref=back.at[it, pl.ds(segment * QUARTER, QUARTER)],
            send_sem=c_send.at[it],
            recv_sem=c_recv.at[it],
            device_id=at_mem(lax.rem(mm + k, MEMS)),
            device_id_type=MESH,
        )

    def start_back(it):
        for k in (2, 1, 3):
            back_copy(it, k).start()
        back[it, pl.ds(segment * QUARTER, QUARTER)] = zs[it]

    def wait_back(it):
        wait_bytes(back.at[it, 0 : 3 * QUARTER], c_recv.at[it])
        wait_bytes(back.at[it, 0 : 3 * QUARTER], c_send.at[it])

    def gather_back(it):
        wide = jnp.concatenate([back[it, 16 * q : 16 * q + 16].reshape(256, 128) for q in range(4)], axis=1)
        for s in range(STENCIL):
            hs[s] = lax.dot_general(
                onehot[s * 512 : s * 512 + 512, :], wide, (((1,), (1,)), ((), ())), preferred_element_type=F32
            ).astype(BF16)

    def prolong(piece):
        total = None
        for s in range(STENCIL):
            term = lax.dot_general(
                hs[s],
                wv[s, piece * 256 : piece * 256 + 256, :],
                (((1,), (1,)), ((), ())),
                preferred_element_type=F32,
            )
            total = term if total is None else total + term
        return total

    loads[9].wait()
    loads[10].wait()
    lax.fori_loop(0, LOCAL, turn, 0)
    pl.semaphore_wait(barrier, TILES - 1 + MEMS - 1)

    def send_halo(m, carry):
        halo_copy(0, m).start()
        halo_copy(1, m).start()
        return carry

    lax.fori_loop(0, LOCAL, send_halo, 0)
    for k in range(1, MEMS):
        pl.semaphore_signal(ready, inc=1, device_id=at_mem(lax.rem(mm + k, MEMS)), device_id_type=MESH)
    for r in range(4):
        loads[r].wait()
        fill_blocks(r, bv[r].astype(BF16))
    loads[4].wait()
    for load in loads[11:]:
        load.wait()
    restrict(0)
    start_c(0)
    for r in range(4):
        loads[5 + r].wait()
    square = jnp.zeros((1, 128), F32)
    diag = jnp.zeros((1, 128), F32)
    for r in range(4):
        v = bv[r]
        square = square + pack_row(v * v)
        diag = diag + pack_row(v * v * (1.0 + sv[r]))
    sum_start(0, 0, stack_rows([square, diag]))
    build()
    wait_halo()
    pl.semaphore_wait(ready, MEMS - 1)
    ensemble(0)

    def col_dot(c_it):
        return pack_row(ens[...] * recv_c[c_it, :, 0:16, :].astype(F32))

    sum_start(1, 0, stack_rows([col_dot(0)]))
    sum_start(0, 1, sum_end(0, 0))
    wait_c(0)
    sum_start(1, 1, sum_end(1, 0))
    wait_rs(0)
    start_back(0)
    first_sums = sum_end(0, 1)
    second_sums = sum_end(1, 1)
    rr = pick(first_sums, 0)
    dad = pick(first_sums, 1) + pick(second_sums, 0)
    alpha = rr / dad
    wait_back(0)
    gather_back(0)
    square = jnp.zeros((1, 128), F32)
    diag = jnp.zeros((1, 128), F32)
    cross = jnp.zeros((1, 128), F32)
    for piece in range(4):
        rr_, half = piece // 2, piece % 2
        total = prolong(piece)
        for p in range(2):
            for q in range(4):
                r = 2 * p + rr_
                cols = slice(q * 512 + half * 256, q * 512 + half * 256 + 256)
                j = 4 * p + q
                d = bv[r, :, cols]
                factor = 1.0 + sv[r, :, cols]
                image = d * factor + total[j * 64 : j * 64 + 64, :]
                ab[r, :, cols] = image
                rnew = d - alpha * image
                fb[j, :, piece * 256 : piece * 256 + 256] = rnew.astype(BF16)
                square = square + pack_row(rnew * rnew)
                diag = diag + pack_row(rnew * rnew * factor)
                cross = cross + pack_row(d * rnew * factor)
    sum_start(2, 0, stack_rows([square, diag, cross]))
    restrict(1)
    start_c(1)
    ensemble(1)
    sum_start(3, 0, stack_rows([col_dot(1), col_dot(0)]))
    sum_start(2, 1, sum_end(2, 0))
    wait_c(1)
    sum_start(3, 1, sum_end(3, 0))
    wait_rs(1)
    start_back(1)
    third_sums = sum_end(2, 1)
    fourth_sums = sum_end(3, 1)
    new = pick(third_sums, 0)
    beta = new / rr
    both = pick(third_sums, 2) + pick(fourth_sums, 1)
    dad2 = pick(third_sums, 1) + pick(fourth_sums, 0) + 2.0 * beta * both + beta * beta * dad
    alpha2 = new / dad2
    wait_back(1)
    gather_back(1)
    stores = []
    for piece in range(4):
        rr_, half = piece // 2, piece % 2
        total = prolong(piece)
        for p in range(2):
            for q in range(4):
                r = 2 * p + rr_
                cols = slice(q * 512 + half * 256, q * 512 + half * 256 + 256)
                j = 4 * p + q
                d = bv[r, :, cols]
                image = ab[r, :, cols]
                rnew = d - alpha * image
                second = rnew * (1.0 + sv[r, :, cols]) + total[j * 64 : j * 64 + 64, :] + beta * image
                outv[0, r, :, cols] = alpha * d + alpha2 * (rnew + beta * d)
                outv[1, r, :, cols] = rnew - alpha2 * second
        if half == 1:
            for r in (rr_, 2 + rr_):
                stores.append(pltpu.make_async_copy(outv.at[0, r], sol_hbm.at[:, r, :], out_sem.at[r]))
                stores.append(pltpu.make_async_copy(outv.at[1, r], res_hbm.at[:, r, :], out_sem.at[4 + r]))
                stores[-2].start()
                stores[-1].start()
    for store in stores:
        store.wait()


def place(a_ref, b_ref, sol_ref, res_ref, held, in_sems, out_sems):
    reads, writes = [], []
    for part in range(4):
        rows = pl.ds(16 * part, 16)
        for n, (source, target) in enumerate(((a_ref, sol_ref), (b_ref, res_ref))):
            reads.append(pltpu.make_async_copy(source.at[rows], held.at[n, rows], in_sems.at[n, part]))
            writes.append(pltpu.make_async_copy(held.at[n, rows], target.at[rows], out_sems.at[n, part]))
    for read in reads:
        read.start()
    for read, write in zip(reads, writes):
        read.wait()
        write.start()
    for write in writes:
        write.wait()


def on_device(right_side, static_var, members, vertical_root, stencil, weights):
    coef = np.repeat(row_blocks().reshape(44, 4), LEV, axis=1)
    coef = jnp.asarray(np.concatenate([coef, np.zeros((4, 256))]), F32)
    order = np.zeros((ROWS, ROWS))
    for i in range(2):
        for par in range(2):
            for pair in range(PAIRS):
                order[i * 64 + par * PAIRS + pair, 4 * pair + 2 * par + i] = 1.0
    perm = jnp.asarray(order, BF16)
    xop = jnp.asarray(column_operator(), BF16)
    anyspec = pl.BlockSpec(memory_space=pl.ANY)
    field = jax.ShapeDtypeStruct(right_side.shape, F32)
    fields = pl.pallas_call(
        kernel,
        out_shape=(field, field),
        in_specs=[anyspec] * 9,
        out_specs=(anyspec, anyspec),
        scratch_shapes=[
            pltpu.VMEM((LEV, LEV), F32),
            pltpu.VMEM((48, 256), F32),
            pltpu.VMEM((128, 256), BF16),
            pltpu.VMEM((128, 128), BF16),
            pltpu.SMEM((STENCIL, 8), jnp.int32),
            pltpu.VMEM((4, LEV, 2048), F32),
            pltpu.VMEM((4, LEV, 2048), F32),
            pltpu.VMEM((4, LEV, 2048), F32),
            pltpu.VMEM((LOCAL, LEV, WIDTH, 128), BF16),
            pltpu.VMEM((COLS, 128), F32),
            pltpu.VMEM((COLS, 128), F32),
            pltpu.VMEM((2, LOCAL, PAIRS, 16, 128), BF16),
            pltpu.VMEM((2, LOCAL, PAIRS, 16, 128), BF16),
            pltpu.VMEM((LOCAL, TILES, 32, 128), BF16),
            pltpu.VMEM((11 * 256, 256), BF16),
            pltpu.VMEM((STENCIL, 1024, 256), BF16),
            pltpu.VMEM((8, LEV, 1024), BF16),
            pltpu.VMEM((2048, 512), BF16),
            pltpu.VMEM((2, TILES, 32, 128), BF16),
            pltpu.VMEM((2, TILES, 32, 128), BF16),
            pltpu.VMEM((COLS, 128), F32),
            pltpu.VMEM((LOCAL, 576, 256), BF16),
            pltpu.VMEM((TILES, 16, 128), F32),
            pltpu.VMEM((2, TILES, 16, 128), BF16),
            pltpu.VMEM((2, MEMS, QUARTER, 16, 128), BF16),
            pltpu.VMEM((2, QUARTER, 16, 128), BF16),
            pltpu.VMEM((2, TILES, 16, 128), BF16),
            pltpu.VMEM((STENCIL, 512, 256), BF16),
            pltpu.VMEM((2, 4, LEV, 2048), F32),
            pltpu.VMEM((4, 2, 8, 128), F32),
            pltpu.VMEM((4, 2, 16, 8, 128), F32),
            pltpu.SemaphoreType.DMA((15,)),
            pltpu.SemaphoreType.DMA((2,)),
            pltpu.SemaphoreType.DMA((2, 4)),
            pltpu.SemaphoreType.DMA((2,)),
            pltpu.SemaphoreType.DMA((2,)),
            pltpu.SemaphoreType.DMA((2,)),
            pltpu.SemaphoreType.DMA((2,)),
            pltpu.SemaphoreType.DMA((4, 2)),
            pltpu.SemaphoreType.DMA((4, 2)),
            pltpu.SemaphoreType.DMA((2,)),
            pltpu.SemaphoreType.DMA((2,)),
            pltpu.SemaphoreType.REGULAR,
            pltpu.SemaphoreType.DMA((8,)),
        ],
        compiler_params=pltpu.CompilerParams(
            collective_id=0, has_side_effects=True, vmem_limit_bytes=58 * 1024 * 1024
        ),
        name="conjugate_gradient",
    )(right_side, static_var, members, vertical_root, coef, xop, perm, stencil.T, weights)
    return pl.pallas_call(
        place,
        out_shape=(field, field),
        in_specs=[anyspec] * 2,
        out_specs=(anyspec, anyspec),
        scratch_shapes=[
            pltpu.VMEM((2,) + right_side.shape, F32),
            pltpu.SemaphoreType.DMA((2, 4)),
            pltpu.SemaphoreType.DMA((2, 4)),
        ],
        compiler_params=pltpu.CompilerParams(vmem_limit_bytes=58 * 1024 * 1024),
        name="outputs",
    )(*fields)


def solution(mesh):
    in_specs = (
        P(None, "tile", None),
        P(None, "tile", None),
        P("mem", None, "tile", None),
        P(),
        P("tile", None),
        P(),
    )
    out_specs = (P(None, "tile", None), P(None, "tile", None))
    return jax.shard_map(on_device, mesh=mesh, in_specs=in_specs, out_specs=out_specs, check_vma=False)
```

```python
import functools
import math

import jax
import jax.numpy as jnp
import numpy as np
from jax import lax
from jax.experimental import pallas as pl
from jax.experimental.pallas import tpu as pltpu
from jax.sharding import PartitionSpec as P

LEV = 64
COLS = 1024
BLOCK = 256
STENCIL = 4
REACH = 4
MEMBERS = 20
ROWS = 128
TILES = 64
MEMS = 4
LOCAL = 5
WIDTH = 16
QUARTER = TILES // MEMS
PAIRS = 32
MESH = pl.DeviceIdType.MESH
F32 = jnp.float32
BF16 = jnp.bfloat16


def kernel_taps(reach):
    values = [math.exp(-(offset * offset) / (reach * reach)) for offset in range(-reach, reach + 1)]
    summed = sum(values)
    return np.array([factor / summed for factor in values])


def row_operator():
    taps = kernel_taps(REACH)
    once = np.zeros((ROWS, ROWS))
    for row in range(ROWS):
        for offset in range(-REACH, REACH + 1):
            if 0 <= row + offset < ROWS:
                once[row, row + offset] = taps[offset + REACH]
    return once @ once


def row_blocks():
    twice = row_operator()
    kinds = []
    for group, shifts in ((8, range(-2, 3)), (0, range(0, 3)), (31, range(-2, 1))):
        for shift in shifts:
            at = 4 * (group + shift)
            kinds.append(twice[4 * group : 4 * group + 4, at : at + 4].T)
    return np.stack(kinds)


def column_operator():
    taps = kernel_taps(REACH)
    twice = np.convolve(taps, taps)
    places = list(range(WIDTH)) + list(range(-8, 0)) + list(range(WIDTH, WIDTH + 8))
    out = np.zeros((WIDTH, 2 * WIDTH))
    for to in range(WIDTH):
        for at, place in enumerate(places):
            if abs(place - to) <= 2 * REACH:
                out[to, at] = twice[place - to + 2 * REACH]
    return np.kron(np.eye(8), out)


def kernel(
    b_hbm, s_hbm, mem_hbm, root_hbm, coef_hbm, xop_hbm, perm_hbm, st_hbm, w_hbm, sol_hbm, res_hbm,
    root_ref, coef_ref, xop, perm, st_ref, bv, sv, ab, mraw, wide_t, wide_g, halo_send, halo_recv, mem, amat, wv, fb, onehot, send_c, recv_c, own_c, u, ens, es, rs, zs, back, hs, outv,
    part, sums,
    load_sem, a_send, a_recv, b_send, b_recv, c_send, c_recv, s_send, s_recv, h_send, h_recv, ready, out_sem,
):
    me = lax.axis_index("tile")
    mm = lax.axis_index("mem")

    def wait_bytes(ref, sem):
        pltpu.make_async_copy(ref, ref, sem).wait()

    def at_tile(t):
        return {"tile": t, "mem": mm}

    def at_mem(m):
        return {"tile": me, "mem": m}

    loads = []
    for r in range(4):
        loads.append(pltpu.make_async_copy(b_hbm.at[:, r, :], bv.at[r], load_sem.at[r]))
    loads.append(pltpu.make_async_copy(w_hbm, wv, load_sem.at[4]))
    for r in range(4):
        loads.append(pltpu.make_async_copy(s_hbm.at[:, r, :], sv.at[r], load_sem.at[5 + r]))
    loads.append(pltpu.make_async_copy(mem_hbm, mraw, load_sem.at[9]))
    loads.append(pltpu.make_async_copy(perm_hbm, perm, load_sem.at[10]))
    loads.append(pltpu.make_async_copy(st_hbm, st_ref, load_sem.at[11]))
    loads.append(pltpu.make_async_copy(root_hbm, root_ref, load_sem.at[12]))
    loads.append(pltpu.make_async_copy(coef_hbm, coef_ref, load_sem.at[13]))
    loads.append(pltpu.make_async_copy(xop_hbm, xop, load_sem.at[14]))
    for load in loads[9:11]:
        load.start()
    barrier = pltpu.get_barrier_semaphore()

    def greet(k, carry):
        pl.semaphore_signal(barrier, inc=1, device_id=at_tile(lax.rem(me + k, TILES)), device_id_type=MESH)
        return carry

    lax.fori_loop(1, TILES, greet, 0)
    for k in range(1, MEMS):
        pl.semaphore_signal(barrier, inc=1, device_id=at_mem(lax.rem(mm + k, MEMS)), device_id_type=MESH)
    for load in loads[:9] + loads[11:]:
        load.start()

    def build():
        rows_at = lax.broadcasted_iota(jnp.int32, (LEV, 2 * LEV), 0)
        lanes_at = lax.broadcasted_iota(jnp.int32, (LEV, 2 * LEV), 1)
        eye0 = (lanes_at == rows_at).astype(F32)
        eye1 = (lanes_at == rows_at + LEV).astype(F32)
        for s in range(STENCIL):
            for q in range(4):
                e0 = st_ref[s, q]
                e1 = st_ref[s, 4 + q]

                def place(j, carry, s=s, q=q, e0=e0, e1=e1):
                    h0 = jnp.where(e0 == j, 1.0, 0.0).astype(F32)
                    h1 = jnp.where(e1 == j, 1.0, 0.0).astype(F32)
                    onehot[pl.ds(pl.multiple_of((s * 8 + j) * LEV, LEV), LEV), q * 128 : q * 128 + 128] = (
                        eye0 * h0 + eye1 * h1
                    ).astype(BF16)
                    return carry

                lax.fori_loop(0, 8, place, 0)
        for m in range(LOCAL):
            u[m, 0:32, :] = jnp.zeros((32, 256), BF16)
            u[m, 544:576, :] = jnp.zeros((32, 256), BF16)
        both = lax.dot_general(
            root_ref[...],
            root_ref[...],
            (((1,), (1,)), ((), ())),
            preferred_element_type=F32,
            precision=lax.Precision.HIGHEST,
        ) * (1.0 / (MEMBERS - 1))
        four = jnp.concatenate([both] * 4, axis=1)

        def scale(n, carry):
            amat[pl.ds(pl.multiple_of(n * LEV, LEV), LEV), :] = (four * coef_ref[pl.ds(n, 1), :]).astype(BF16)
            return carry

        lax.fori_loop(0, 44, scale, 0)

    def halo_copy(side, m):
        to = lax.rem(me + (TILES - 1 if side == 0 else 1), TILES)
        return pltpu.make_async_remote_copy(
            src_ref=halo_send.at[side, m],
            dst_ref=halo_recv.at[side, m],
            send_sem=h_send.at[side],
            recv_sem=h_recv.at[side],
            device_id=at_tile(to),
            device_id_type=MESH,
        )

    def turn(m, carry):
        wide_t[...] = mraw[m].reshape(COLS, 128).astype(F32)
        for c in range(WIDTH):
            at = wide_t[pl.ds(c, LEV, stride=WIDTH), :].astype(BF16)
            rows = lax.dot_general(perm[...], at, (((1,), (1,)), ((), ())), preferred_element_type=F32)
            wide_g[pl.ds(c, TILES, stride=WIDTH), :] = jnp.concatenate([rows[:64], rows[64:]], axis=1)
        turned = wide_g[...]
        mem[m, :, 0:16, :] = turned.reshape(TILES, 16, 128).astype(BF16)
        halves = turned.reshape(TILES, 2, 8, 128)
        for side in range(2):
            halo_send[side, m] = halves[:, side].reshape(PAIRS, 16, 128).astype(BF16)
        return carry

    def wait_halo():
        for side in range(2):
            wait_bytes(halo_recv.at[side], h_recv.at[side])
            wait_bytes(halo_send.at[side], h_send.at[side])

        def join(m, carry):
            before = halo_recv[1, m].astype(F32).reshape(TILES, 8, 128)
            after = halo_recv[0, m].astype(F32).reshape(TILES, 8, 128)
            mem[m, :, 16:32, :] = jnp.concatenate([before, after], axis=1).astype(BF16)
            return carry

        lax.fori_loop(0, LOCAL, join, 0)

    def pack_row(v):
        return jnp.sum(v.reshape(-1, 8, 128), axis=0).sum(axis=0, keepdims=True)

    def restrict(it):
        acc = None
        for s in range(STENCIL):
            rows = []
            for q in range(4):
                for i in range(2):
                    rows.append(fb[st_ref[s, 4 * i + q]])
            term = jnp.dot(jnp.concatenate(rows, axis=0), wv[s], preferred_element_type=F32)
            acc = term if acc is None else acc + term
        for q in range(4):
            turned = acc[q * 128 : q * 128 + 128].T
            own_c[q * 256 : q * 256 + 256, :] = turned
        grid = own_c[...].reshape(TILES, 2, 8, 128)
        first, last = grid[:, 0], grid[:, 1]
        before = jnp.concatenate([last[TILES - 1 :], last[: TILES - 1]], axis=0)
        after = jnp.concatenate([first[1:], first[:1]], axis=0)
        send_c[it, :, 0:16, :] = jnp.concatenate([first, last], axis=1).astype(BF16)
        send_c[it, :, 16:32, :] = jnp.concatenate([before, after], axis=1).astype(BF16)

    def fill_blocks(r, field):
        p, rr = r // 2, r % 2
        for q in range(4):
            fb[4 * p + q, :, rr * 512 : rr * 512 + 512] = field[:, q * 512 : q * 512 + 512]

    group_of_me = lax.div(me, QUARTER)
    mine = lax.rem(me, 2) * PAIRS + lax.div(me, 2)


    def c_copy(it, t):
        return pltpu.make_async_remote_copy(
            src_ref=send_c.at[it, t],
            dst_ref=recv_c.at[it, mine],
            send_sem=a_send.at[it],
            recv_sem=a_recv.at[it, group_of_me],
            device_id=at_tile(t),
            device_id_type=MESH,
        )

    def start_c(it):
        def go(k, carry):
            c_copy(it, lax.rem(me + k, TILES)).start()
            return carry

        lax.fori_loop(1, TILES, go, 0)
        pltpu.make_async_copy(send_c.at[it, me], recv_c.at[it, mine], a_recv.at[it, group_of_me]).start()

    def wait_c(it):
        wait_bytes(send_c.at[it, 0 : TILES - 1], a_send.at[it])

    def sum_peers(x):
        return 16 if x % 2 else 8

    def sum_place(x, stage):
        if x % 2:
            return mm * 4 + lax.rem(me, 4) if stage == 0 else lax.div(me, 4)
        return lax.rem(me, 8) if stage == 0 else lax.div(me, 8)

    def sum_copy(x, stage, k):
        peer = lax.rem(sum_place(x, stage) + k, sum_peers(x))
        if x % 2:
            if stage == 0:
                to = {"tile": lax.div(me, 4) * 4 + lax.rem(peer, 4), "mem": lax.div(peer, 4)}
            else:
                to = at_tile(peer * 4 + lax.rem(me, 4))
        else:
            to = at_tile(lax.div(me, 8) * 8 + peer if stage == 0 else peer * 8 + lax.rem(me, 8))
        return pltpu.make_async_remote_copy(
            src_ref=part.at[x, stage],
            dst_ref=sums.at[x, stage, sum_place(x, stage)],
            send_sem=s_send.at[x, stage],
            recv_sem=s_recv.at[x, stage],
            device_id=to,
            device_id_type=MESH,
        )

    def sum_start(x, stage, value):
        part[x, stage] = value
        sums[x, stage, sum_place(x, stage)] = value

        def go(k, carry):
            sum_copy(x, stage, k).start()
            return carry

        lax.fori_loop(1, sum_peers(x), go, 0)

    def sum_end(x, stage):
        wait_bytes(sums.at[x, stage, 0 : sum_peers(x) - 1], s_recv.at[x, stage])
        wait_bytes(sums.at[x, stage, 0 : sum_peers(x) - 1], s_send.at[x, stage])
        return jnp.sum(sums[x, stage, 0 : sum_peers(x)], axis=0)

    def stack_rows(rows):
        rows = rows + [jnp.zeros((8 - len(rows), 128), F32)]
        return jnp.concatenate(rows, axis=0)

    def pick(tile, row):
        return jnp.sum(tile[row : row + 1, :], axis=1, keepdims=True)

    def mix(it):
        def group(turn_at, carry):
            g = lax.rem(group_of_me + 3 - turn_at, 4)
            wait_bytes(recv_c.at[it, 0:QUARTER], a_recv.at[it, g])
            for m in range(LOCAL):
                lanes = []
                for par in range(2):
                    at = par * PAIRS + 8 * g
                    lanes.append((mem[m, pl.ds(at, 8)] * recv_c[it, pl.ds(at, 8)]).reshape(256, 128))
                mixed = jnp.dot(xop[...], jnp.concatenate(lanes, axis=1), preferred_element_type=F32)
                u[m, pl.ds(pl.multiple_of(32 + 128 * g, 32), 128), :] = mixed.astype(BF16)
            return carry

        lax.fori_loop(0, 4, group, 0)

    def own_part(m, at, count):
        return mem[m, pl.ds(at, count), 0:16, :].astype(F32)

    to_self = lax.rem(group_of_me + me, MEMS) == mm
    segment = lax.rem(mm + TILES - me, MEMS)
    slot = lax.rem(me, QUARTER)

    def out_go(it, t):
        itself = jnp.logical_and(t == me, to_self)

        @pl.when(jnp.logical_not(itself))
        def _():
            pltpu.make_async_remote_copy(
                src_ref=es.at[it, t],
                dst_ref=rs.at[it, mm, slot],
                send_sem=b_send.at[it],
                recv_sem=b_recv.at[it],
                device_id={"tile": t, "mem": lax.rem(group_of_me + t, MEMS)},
                device_id_type=MESH,
            ).start()

        @pl.when(itself)
        def _():
            pltpu.make_async_copy(es.at[it, t], rs.at[it, mm, slot], b_recv.at[it]).start()

    def send_group(it, turn_at):
        g = lax.rem(group_of_me + mm + 1 + turn_at, 4)

        def go(k, carry):
            out_go(it, g * QUARTER + lax.rem(me + k, QUARTER))
            return carry

        lax.fori_loop(0, QUARTER, go, 0)

    def ensemble(it):
        mix(it)

        def group(turn_at, carry):
            g = lax.rem(group_of_me + mm + 1 + turn_at, 4)
            wide = []
            for m in range(LOCAL):
                pieces = []
                for d in range(-2, 3):
                    pieces.append(u[m, pl.ds(pl.multiple_of(32 + 128 * g + 16 * d, 16), 128), :])
                wide.append(jnp.concatenate(pieces, axis=1))
            inner = jnp.dot(jnp.concatenate(wide, axis=0), amat[0:1280, :], preferred_element_type=F32)
            for par in range(2):
                total = jnp.zeros((8, 16, 128), F32)
                for m in range(LOCAL):
                    term = inner[m * 128 : m * 128 + 128, par * 128 : par * 128 + 128].reshape(8, 16, 128)
                    total = total + own_part(m, par * PAIRS + 8 * g, 8) * term
                ens[pl.ds(par * PAIRS + 8 * g, 8)] = total

            def edge(pair, shifts, at):
                wide = []
                for m in range(LOCAL):
                    wide.append(
                        jnp.concatenate([u[m, 32 + 16 * (pair + d) : 48 + 16 * (pair + d), :] for d in shifts], axis=1)
                    )
                inner = jnp.dot(
                    jnp.concatenate(wide, axis=0), amat[at : at + 768, :], preferred_element_type=F32
                )
                for par in range(2):
                    total = jnp.zeros((1, 16, 128), F32)
                    for m in range(LOCAL):
                        term = inner[m * 16 : m * 16 + 16, par * 128 : par * 128 + 128].reshape(1, 16, 128)
                        total = total + own_part(m, par * PAIRS + pair, 1) * term
                    ens[par * PAIRS + pair : par * PAIRS + pair + 1] = total

            @pl.when(g == 0)
            def _():
                edge(0, range(0, 3), 1280)

            @pl.when(g == 3)
            def _():
                edge(PAIRS - 1, range(-2, 1), 2048)

            even = ens[pl.ds(8 * g, 8)]
            odd = ens[pl.ds(PAIRS + 8 * g, 8)]
            both = jnp.stack([even, odd], axis=1).reshape(QUARTER, 16, 128).astype(BF16)
            es[it, pl.ds(g * QUARTER, QUARTER)] = both

            @pl.when(turn_at < 3)
            def _():
                send_group(it, turn_at)

            return carry

        lax.fori_loop(0, MEMS, group, 0)

    def wait_rs(it):
        wait_bytes(es.at[it], b_recv.at[it])

        @pl.when(to_self)
        def _():
            wait_bytes(es.at[it, 0 : TILES - 1], b_send.at[it])

        @pl.when(jnp.logical_not(to_self))
        def _():
            wait_bytes(es.at[it], b_send.at[it])

        total = rs[it, 0].astype(F32)
        for m in range(1, MEMS):
            total = total + rs[it, m].astype(F32)
        zs[it] = total.astype(BF16)

    def back_copy(it, k):
        return pltpu.make_async_remote_copy(
            src_ref=zs.at[it],
            dst_ref=back.at[it, pl.ds(segment * QUARTER, QUARTER)],
            send_sem=c_send.at[it],
            recv_sem=c_recv.at[it],
            device_id=at_mem(lax.rem(mm + k, MEMS)),
            device_id_type=MESH,
        )

    def start_back(it):
        for k in (2, 1, 3):
            back_copy(it, k).start()
        back[it, pl.ds(segment * QUARTER, QUARTER)] = zs[it]

    def wait_back(it):
        wait_bytes(back.at[it, 0 : 3 * QUARTER], c_recv.at[it])
        wait_bytes(back.at[it, 0 : 3 * QUARTER], c_send.at[it])

    def gather_back(it):
        wide = jnp.concatenate([back[it, 16 * q : 16 * q + 16].reshape(256, 128) for q in range(4)], axis=1)
        for s in range(STENCIL):
            hs[s] = lax.dot_general(
                onehot[s * 512 : s * 512 + 512, :], wide, (((1,), (1,)), ((), ())), preferred_element_type=F32
            ).astype(BF16)

    def prolong(piece):
        total = None
        for s in range(STENCIL):
            term = lax.dot_general(
                hs[s],
                wv[s, piece * 256 : piece * 256 + 256, :],
                (((1,), (1,)), ((), ())),
                preferred_element_type=F32,
            )
            total = term if total is None else total + term
        return total

    loads[9].wait()
    loads[10].wait()
    lax.fori_loop(0, LOCAL, turn, 0)
    pl.semaphore_wait(barrier, TILES - 1 + MEMS - 1)

    def send_halo(m, carry):
        halo_copy(0, m).start()
        halo_copy(1, m).start()
        return carry

    lax.fori_loop(0, LOCAL, send_halo, 0)
    for k in range(1, MEMS):
        pl.semaphore_signal(ready, inc=1, device_id=at_mem(lax.rem(mm + k, MEMS)), device_id_type=MESH)
    for r in range(4):
        loads[r].wait()
        fill_blocks(r, bv[r].astype(BF16))
    loads[4].wait()
    for load in loads[11:]:
        load.wait()
    restrict(0)
    start_c(0)
    for r in range(4):
        loads[5 + r].wait()
    square = jnp.zeros((1, 128), F32)
    diag = jnp.zeros((1, 128), F32)
    for r in range(4):
        v = bv[r]
        square = square + pack_row(v * v)
        diag = diag + pack_row(v * v * (1.0 + sv[r]))
    sum_start(0, 0, stack_rows([square, diag]))
    build()
    wait_halo()
    pl.semaphore_wait(ready, MEMS - 1)
    ensemble(0)

    def col_dot(c_it):
        return pack_row(ens[...] * recv_c[c_it, :, 0:16, :].astype(F32))

    sum_start(1, 0, stack_rows([col_dot(0)]))
    send_group(0, 3)
    sum_start(0, 1, sum_end(0, 0))
    wait_c(0)
    sum_start(1, 1, sum_end(1, 0))
    wait_rs(0)
    start_back(0)
    first_sums = sum_end(0, 1)
    second_sums = sum_end(1, 1)
    rr = pick(first_sums, 0)
    dad = pick(first_sums, 1) + pick(second_sums, 0)
    alpha = rr / dad
    for r in range(4):
        ab[r] = bv[r] * (1.0 + sv[r])
    wait_back(0)
    gather_back(0)
    square = jnp.zeros((1, 128), F32)
    diag = jnp.zeros((1, 128), F32)
    cross = jnp.zeros((1, 128), F32)
    for piece in range(4):
        rr_, half = piece // 2, piece % 2
        total = prolong(piece)
        for p in range(2):
            for q in range(4):
                r = 2 * p + rr_
                cols = slice(q * 512 + half * 256, q * 512 + half * 256 + 256)
                j = 4 * p + q
                d = bv[r, :, cols]
                factor = 1.0 + sv[r, :, cols]
                image = ab[r, :, cols] + total[j * 64 : j * 64 + 64, :]
                ab[r, :, cols] = image
                rnew = d - alpha * image
                fb[j, :, piece * 256 : piece * 256 + 256] = rnew.astype(BF16)
                square = square + pack_row(rnew * rnew)
                diag = diag + pack_row(rnew * rnew * factor)
                cross = cross + pack_row(d * rnew * factor)
    sum_start(2, 0, stack_rows([square, diag, cross]))
    restrict(1)
    start_c(1)
    ensemble(1)
    sum_start(3, 0, stack_rows([col_dot(1), col_dot(0)]))
    send_group(1, 3)
    sum_start(2, 1, sum_end(2, 0))
    wait_c(1)
    sum_start(3, 1, sum_end(3, 0))
    wait_rs(1)
    start_back(1)
    third_sums = sum_end(2, 1)
    fourth_sums = sum_end(3, 1)
    new = pick(third_sums, 0)
    beta = new / rr
    both = pick(third_sums, 2) + pick(fourth_sums, 1)
    dad2 = pick(third_sums, 1) + pick(fourth_sums, 0) + 2.0 * beta * both + beta * beta * dad
    alpha2 = new / dad2
    stores = []
    for r in range(4):
        d = bv[r]
        image = ab[r]
        rnew = d - alpha * image
        outv[0, r] = alpha * d + alpha2 * (rnew + beta * d)
        outv[1, r] = rnew - alpha2 * (rnew * (1.0 + sv[r]) + beta * image)
        stores.append(pltpu.make_async_copy(outv.at[0, r], sol_hbm.at[:, r, :], out_sem.at[r]))
        stores[-1].start()
    wait_back(1)
    gather_back(1)
    for piece in range(4):
        rr_, half = piece // 2, piece % 2
        total = prolong(piece)
        for p in range(2):
            for q in range(4):
                r = 2 * p + rr_
                cols = slice(q * 512 + half * 256, q * 512 + half * 256 + 256)
                j = 4 * p + q
                outv[1, r, :, cols] = outv[1, r, :, cols] - alpha2 * total[j * 64 : j * 64 + 64, :]
        if half == 1:
            for r in (rr_, 2 + rr_):
                stores.append(pltpu.make_async_copy(outv.at[1, r], res_hbm.at[:, r, :], out_sem.at[4 + r]))
                stores[-1].start()
    for store in stores:
        store.wait()


def place(a_ref, b_ref, sol_ref, res_ref, held, in_sems, out_sems):
    reads, writes = [], []
    for part in range(2):
        rows = pl.ds(32 * part, 32)
        for n, (source, target) in enumerate(((a_ref, sol_ref), (b_ref, res_ref))):
            reads.append(pltpu.make_async_copy(source.at[rows], held.at[n, rows], in_sems.at[n, part]))
            writes.append(pltpu.make_async_copy(held.at[n, rows], target.at[rows], out_sems.at[n, part]))
    for read in reads:
        read.start()
    for read, write in zip(reads, writes):
        read.wait()
        write.start()
    for write in writes:
        write.wait()


def on_device(right_side, static_var, members, vertical_root, stencil, weights):
    coef = np.repeat(row_blocks().reshape(44, 4), LEV, axis=1)
    coef = jnp.asarray(np.concatenate([coef, np.zeros((4, 256))]), F32)
    order = np.zeros((ROWS, ROWS))
    for i in range(2):
        for par in range(2):
            for pair in range(PAIRS):
                order[i * 64 + par * PAIRS + pair, 4 * pair + 2 * par + i] = 1.0
    perm = jnp.asarray(order, BF16)
    xop = jnp.asarray(column_operator(), BF16)
    anyspec = pl.BlockSpec(memory_space=pl.ANY)
    field = jax.ShapeDtypeStruct(right_side.shape, F32)
    fields = pl.pallas_call(
        kernel,
        out_shape=(field, field),
        in_specs=[anyspec] * 9,
        out_specs=(anyspec, anyspec),
        scratch_shapes=[
            pltpu.VMEM((LEV, LEV), F32),
            pltpu.VMEM((48, 256), F32),
            pltpu.VMEM((128, 256), BF16),
            pltpu.VMEM((128, 128), BF16),
            pltpu.SMEM((STENCIL, 8), jnp.int32),
            pltpu.VMEM((4, LEV, 2048), F32),
            pltpu.VMEM((4, LEV, 2048), F32),
            pltpu.VMEM((4, LEV, 2048), F32),
            pltpu.VMEM((LOCAL, LEV, WIDTH, 128), BF16),
            pltpu.VMEM((COLS, 128), F32),
            pltpu.VMEM((COLS, 128), F32),
            pltpu.VMEM((2, LOCAL, PAIRS, 16, 128), BF16),
            pltpu.VMEM((2, LOCAL, PAIRS, 16, 128), BF16),
            pltpu.VMEM((LOCAL, TILES, 32, 128), BF16),
            pltpu.VMEM((11 * 256, 256), BF16),
            pltpu.VMEM((STENCIL, 1024, 256), BF16),
            pltpu.VMEM((8, LEV, 1024), BF16),
            pltpu.VMEM((2048, 512), BF16),
            pltpu.VMEM((2, TILES, 32, 128), BF16),
            pltpu.VMEM((2, TILES, 32, 128), BF16),
            pltpu.VMEM((COLS, 128), F32),
            pltpu.VMEM((LOCAL, 576, 256), BF16),
            pltpu.VMEM((TILES, 16, 128), F32),
            pltpu.VMEM((2, TILES, 16, 128), BF16),
            pltpu.VMEM((2, MEMS, QUARTER, 16, 128), BF16),
            pltpu.VMEM((2, QUARTER, 16, 128), BF16),
            pltpu.VMEM((2, TILES, 16, 128), BF16),
            pltpu.VMEM((STENCIL, 512, 256), BF16),
            pltpu.VMEM((2, 4, LEV, 2048), F32),
            pltpu.VMEM((4, 2, 8, 128), F32),
            pltpu.VMEM((4, 2, 16, 8, 128), F32),
            pltpu.SemaphoreType.DMA((15,)),
            pltpu.SemaphoreType.DMA((2,)),
            pltpu.SemaphoreType.DMA((2, 4)),
            pltpu.SemaphoreType.DMA((2,)),
            pltpu.SemaphoreType.DMA((2,)),
            pltpu.SemaphoreType.DMA((2,)),
            pltpu.SemaphoreType.DMA((2,)),
            pltpu.SemaphoreType.DMA((4, 2)),
            pltpu.SemaphoreType.DMA((4, 2)),
            pltpu.SemaphoreType.DMA((2,)),
            pltpu.SemaphoreType.DMA((2,)),
            pltpu.SemaphoreType.REGULAR,
            pltpu.SemaphoreType.DMA((8,)),
        ],
        compiler_params=pltpu.CompilerParams(
            collective_id=0, has_side_effects=True, vmem_limit_bytes=58 * 1024 * 1024
        ),
        name="conjugate_gradient",
    )(right_side, static_var, members, vertical_root, coef, xop, perm, stencil.T, weights)
    return pl.pallas_call(
        place,
        out_shape=(field, field),
        in_specs=[anyspec] * 2,
        out_specs=(anyspec, anyspec),
        scratch_shapes=[
            pltpu.VMEM((2,) + right_side.shape, F32),
            pltpu.SemaphoreType.DMA((2, 8)),
            pltpu.SemaphoreType.DMA((2, 8)),
        ],
        compiler_params=pltpu.CompilerParams(vmem_limit_bytes=58 * 1024 * 1024),
        name="outputs",
    )(*fields)


def solution(mesh):
    in_specs = (
        P(None, "tile", None),
        P(None, "tile", None),
        P("mem", None, "tile", None),
        P(),
        P("tile", None),
        P(),
    )
    out_specs = (P(None, "tile", None), P(None, "tile", None))
    return jax.shard_map(on_device, mesh=mesh, in_specs=in_specs, out_specs=out_specs, check_vma=False)
```

```python
import functools
import math

import jax
import jax.numpy as jnp
import numpy as np
from jax import lax
from jax.experimental import pallas as pl
from jax.experimental.pallas import tpu as pltpu
from jax.sharding import PartitionSpec as P

LEV = 64
COLS = 1024
BLOCK = 256
STENCIL = 4
REACH = 4
MEMBERS = 20
ROWS = 128
TILES = 64
MEMS = 4
LOCAL = 5
WIDTH = 16
QUARTER = TILES // MEMS
PAIRS = 32
MESH = pl.DeviceIdType.MESH
F32 = jnp.float32
BF16 = jnp.bfloat16


def kernel_taps(reach):
    values = [math.exp(-(offset * offset) / (reach * reach)) for offset in range(-reach, reach + 1)]
    summed = sum(values)
    return np.array([factor / summed for factor in values])


def row_operator():
    taps = kernel_taps(REACH)
    once = np.zeros((ROWS, ROWS))
    for row in range(ROWS):
        for offset in range(-REACH, REACH + 1):
            if 0 <= row + offset < ROWS:
                once[row, row + offset] = taps[offset + REACH]
    return once @ once


def row_blocks():
    twice = row_operator()
    kinds = []
    for group, shifts in ((8, range(-2, 3)), (0, range(0, 3)), (31, range(-2, 1))):
        for shift in shifts:
            at = 4 * (group + shift)
            kinds.append(twice[4 * group : 4 * group + 4, at : at + 4].T)
    return np.stack(kinds)


def column_operator():
    taps = kernel_taps(REACH)
    twice = np.convolve(taps, taps)
    places = list(range(WIDTH)) + list(range(-8, 0)) + list(range(WIDTH, WIDTH + 8))
    out = np.zeros((WIDTH, 2 * WIDTH))
    for to in range(WIDTH):
        for at, place in enumerate(places):
            if abs(place - to) <= 2 * REACH:
                out[to, at] = twice[place - to + 2 * REACH]
    return np.kron(np.eye(8), out)


def kernel(
    b_hbm, s_hbm, mem_hbm, root_hbm, coef_hbm, xop_hbm, perm_hbm, st_hbm, w_hbm, sol_hbm, res_hbm,
    root_ref, coef_ref, xop, perm, st_ref, bv, sv, ab, mraw, wide_t, wide_g, halo_send, halo_recv, mem, amat, wv, fb, onehot, send_c, recv_c, own_c, u, ens, es, rs, zs, back, hs, outv,
    part, sums,
    load_sem, a_send, a_recv, b_send, b_recv, c_send, c_recv, s_send, s_recv, h_send, h_recv, ready, out_sem,
):
    me = lax.axis_index("tile")
    mm = lax.axis_index("mem")

    def wait_bytes(ref, sem):
        pltpu.make_async_copy(ref, ref, sem).wait()

    def at_tile(t):
        return {"tile": t, "mem": mm}

    def at_mem(m):
        return {"tile": me, "mem": m}

    loads = []
    for r in range(4):
        loads.append(pltpu.make_async_copy(b_hbm.at[:, r, :], bv.at[r], load_sem.at[r]))
    loads.append(pltpu.make_async_copy(w_hbm, wv, load_sem.at[4]))
    for r in range(4):
        loads.append(pltpu.make_async_copy(s_hbm.at[:, r, :], sv.at[r], load_sem.at[5 + r]))
    loads.append(pltpu.make_async_copy(mem_hbm, mraw, load_sem.at[9]))
    loads.append(pltpu.make_async_copy(perm_hbm, perm, load_sem.at[10]))
    loads.append(pltpu.make_async_copy(st_hbm, st_ref, load_sem.at[11]))
    loads.append(pltpu.make_async_copy(root_hbm, root_ref, load_sem.at[12]))
    loads.append(pltpu.make_async_copy(coef_hbm, coef_ref, load_sem.at[13]))
    loads.append(pltpu.make_async_copy(xop_hbm, xop, load_sem.at[14]))
    for load in loads[9:11]:
        load.start()
    barrier = pltpu.get_barrier_semaphore()

    def greet(k, carry):
        pl.semaphore_signal(barrier, inc=1, device_id=at_tile(lax.rem(me + k, TILES)), device_id_type=MESH)
        return carry

    lax.fori_loop(1, TILES, greet, 0)
    for k in range(1, MEMS):
        pl.semaphore_signal(barrier, inc=1, device_id=at_mem(lax.rem(mm + k, MEMS)), device_id_type=MESH)
    for load in loads[:9] + loads[11:]:
        load.start()

    def build():
        rows_at = lax.broadcasted_iota(jnp.int32, (LEV, 2 * LEV), 0)
        lanes_at = lax.broadcasted_iota(jnp.int32, (LEV, 2 * LEV), 1)
        eye0 = (lanes_at == rows_at).astype(F32)
        eye1 = (lanes_at == rows_at + LEV).astype(F32)
        for s in range(STENCIL):
            for q in range(4):
                e0 = st_ref[s, q]
                e1 = st_ref[s, 4 + q]

                def place(j, carry, s=s, q=q, e0=e0, e1=e1):
                    h0 = jnp.where(e0 == j, 1.0, 0.0).astype(F32)
                    h1 = jnp.where(e1 == j, 1.0, 0.0).astype(F32)
                    onehot[pl.ds(pl.multiple_of((s * 8 + j) * LEV, LEV), LEV), q * 128 : q * 128 + 128] = (
                        eye0 * h0 + eye1 * h1
                    ).astype(BF16)
                    return carry

                lax.fori_loop(0, 8, place, 0)
        for m in range(LOCAL):
            u[m, 0:32, :] = jnp.zeros((32, 256), BF16)
            u[m, 544:576, :] = jnp.zeros((32, 256), BF16)
        both = lax.dot_general(
            root_ref[...],
            root_ref[...],
            (((1,), (1,)), ((), ())),
            preferred_element_type=F32,
            precision=lax.Precision.HIGHEST,
        ) * (1.0 / (MEMBERS - 1))
        four = jnp.concatenate([both] * 4, axis=1)

        def scale(n, carry):
            amat[pl.ds(pl.multiple_of(n * LEV, LEV), LEV), :] = (four * coef_ref[pl.ds(n, 1), :]).astype(BF16)
            return carry

        lax.fori_loop(0, 44, scale, 0)

    def halo_copy(side, m):
        to = lax.rem(me + (TILES - 1 if side == 0 else 1), TILES)
        return pltpu.make_async_remote_copy(
            src_ref=halo_send.at[side, m],
            dst_ref=halo_recv.at[side, m],
            send_sem=h_send.at[side],
            recv_sem=h_recv.at[side],
            device_id=at_tile(to),
            device_id_type=MESH,
        )

    def turn(m, carry):
        wide_t[...] = mraw[m].reshape(COLS, 128).astype(F32)
        for c in range(WIDTH):
            at = wide_t[pl.ds(c, LEV, stride=WIDTH), :].astype(BF16)
            rows = lax.dot_general(perm[...], at, (((1,), (1,)), ((), ())), preferred_element_type=F32)
            wide_g[pl.ds(c, TILES, stride=WIDTH), :] = jnp.concatenate([rows[:64], rows[64:]], axis=1)
        turned = wide_g[...]
        mem[m, :, 0:16, :] = turned.reshape(TILES, 16, 128).astype(BF16)
        halves = turned.reshape(TILES, 2, 8, 128)
        for side in range(2):
            halo_send[side, m] = halves[:, side].reshape(PAIRS, 16, 128).astype(BF16)
        return carry

    def wait_halo():
        for side in range(2):
            wait_bytes(halo_recv.at[side], h_recv.at[side])
            wait_bytes(halo_send.at[side], h_send.at[side])

        def join(m, carry):
            before = halo_recv[1, m].astype(F32).reshape(TILES, 8, 128)
            after = halo_recv[0, m].astype(F32).reshape(TILES, 8, 128)
            mem[m, :, 16:32, :] = jnp.concatenate([before, after], axis=1).astype(BF16)
            return carry

        lax.fori_loop(0, LOCAL, join, 0)

    def pack_row(v):
        return jnp.sum(v.reshape(-1, 8, 128), axis=0).sum(axis=0, keepdims=True)

    def restrict(it):
        acc = None
        for s in range(STENCIL):
            rows = []
            for q in range(4):
                for i in range(2):
                    rows.append(fb[st_ref[s, 4 * i + q]])
            term = jnp.dot(jnp.concatenate(rows, axis=0), wv[s], preferred_element_type=F32)
            acc = term if acc is None else acc + term
        for q in range(4):
            turned = acc[q * 128 : q * 128 + 128].T
            own_c[q * 256 : q * 256 + 256, :] = turned
        grid = own_c[...].reshape(TILES, 2, 8, 128)
        first, last = grid[:, 0], grid[:, 1]
        before = jnp.concatenate([last[TILES - 1 :], last[: TILES - 1]], axis=0)
        after = jnp.concatenate([first[1:], first[:1]], axis=0)
        send_c[it, :, 0:16, :] = jnp.concatenate([first, last], axis=1).astype(BF16)
        send_c[it, :, 16:32, :] = jnp.concatenate([before, after], axis=1).astype(BF16)

    def fill_blocks(r, field):
        p, rr = r // 2, r % 2
        for q in range(4):
            fb[4 * p + q, :, rr * 512 : rr * 512 + 512] = field[:, q * 512 : q * 512 + 512]

    group_of_me = lax.div(me, QUARTER)
    mine = lax.rem(me, 2) * PAIRS + lax.div(me, 2)


    def c_copy(it, t):
        return pltpu.make_async_remote_copy(
            src_ref=send_c.at[it, t],
            dst_ref=recv_c.at[it, mine],
            send_sem=a_send.at[it],
            recv_sem=a_recv.at[it, group_of_me],
            device_id=at_tile(t),
            device_id_type=MESH,
        )

    def start_c(it):
        def go(k, carry):
            c_copy(it, lax.rem(me + k, TILES)).start()
            return carry

        lax.fori_loop(1, TILES, go, 0)
        pltpu.make_async_copy(send_c.at[it, me], recv_c.at[it, mine], a_recv.at[it, group_of_me]).start()

    def wait_c(it):
        wait_bytes(send_c.at[it, 0 : TILES - 1], a_send.at[it])

    def sum_peers(x):
        return 16 if x % 2 else 8

    def sum_place(x, stage):
        if x % 2:
            return mm * 4 + lax.rem(me, 4) if stage == 0 else lax.div(me, 4)
        return lax.rem(me, 8) if stage == 0 else lax.div(me, 8)

    def sum_copy(x, stage, k):
        peer = lax.rem(sum_place(x, stage) + k, sum_peers(x))
        if x % 2:
            if stage == 0:
                to = {"tile": lax.div(me, 4) * 4 + lax.rem(peer, 4), "mem": lax.div(peer, 4)}
            else:
                to = at_tile(peer * 4 + lax.rem(me, 4))
        else:
            to = at_tile(lax.div(me, 8) * 8 + peer if stage == 0 else peer * 8 + lax.rem(me, 8))
        return pltpu.make_async_remote_copy(
            src_ref=part.at[x, stage],
            dst_ref=sums.at[x, stage, sum_place(x, stage)],
            send_sem=s_send.at[x, stage],
            recv_sem=s_recv.at[x, stage],
            device_id=to,
            device_id_type=MESH,
        )

    def sum_start(x, stage, value):
        part[x, stage] = value
        sums[x, stage, sum_place(x, stage)] = value

        def go(k, carry):
            sum_copy(x, stage, k).start()
            return carry

        lax.fori_loop(1, sum_peers(x), go, 0)

    def sum_end(x, stage):
        wait_bytes(sums.at[x, stage, 0 : sum_peers(x) - 1], s_recv.at[x, stage])
        wait_bytes(sums.at[x, stage, 0 : sum_peers(x) - 1], s_send.at[x, stage])
        return jnp.sum(sums[x, stage, 0 : sum_peers(x)], axis=0)

    def stack_rows(rows):
        rows = rows + [jnp.zeros((8 - len(rows), 128), F32)]
        return jnp.concatenate(rows, axis=0)

    def pick(tile, row):
        return jnp.sum(tile[row : row + 1, :], axis=1, keepdims=True)

    def mix(it):
        def group(turn_at, carry):
            g = lax.rem(group_of_me + 3 - turn_at, 4)
            wait_bytes(recv_c.at[it, 0:QUARTER], a_recv.at[it, g])
            for m in range(LOCAL):
                lanes = []
                for par in range(2):
                    at = par * PAIRS + 8 * g
                    lanes.append((mem[m, pl.ds(at, 8)] * recv_c[it, pl.ds(at, 8)]).reshape(256, 128))
                mixed = jnp.dot(xop[...], jnp.concatenate(lanes, axis=1), preferred_element_type=F32)
                u[m, pl.ds(pl.multiple_of(32 + 128 * g, 32), 128), :] = mixed.astype(BF16)
            return carry

        lax.fori_loop(0, 4, group, 0)

    def own_part(m, at, count):
        return mem[m, pl.ds(at, count), 0:16, :].astype(F32)

    to_self = lax.rem(group_of_me + me, MEMS) == mm
    segment = lax.rem(mm + TILES - me, MEMS)
    slot = lax.rem(me, QUARTER)

    def out_go(it, t):
        itself = jnp.logical_and(t == me, to_self)

        @pl.when(jnp.logical_not(itself))
        def _():
            pltpu.make_async_remote_copy(
                src_ref=es.at[it, t],
                dst_ref=rs.at[it, mm, slot],
                send_sem=b_send.at[it],
                recv_sem=b_recv.at[it],
                device_id={"tile": t, "mem": lax.rem(group_of_me + t, MEMS)},
                device_id_type=MESH,
            ).start()

        @pl.when(itself)
        def _():
            pltpu.make_async_copy(es.at[it, t], rs.at[it, mm, slot], b_recv.at[it]).start()

    def send_group(it, turn_at):
        g = lax.rem(group_of_me + mm + 1 + turn_at, 4)

        def go(k, carry):
            out_go(it, g * QUARTER + lax.rem(me + 5 * k, QUARTER))
            return carry

        lax.fori_loop(0, QUARTER, go, 0)

    def ensemble(it):
        mix(it)

        def group(turn_at, carry):
            g = lax.rem(group_of_me + mm + 1 + turn_at, 4)
            wide = []
            for m in range(LOCAL):
                pieces = []
                for d in range(-2, 3):
                    pieces.append(u[m, pl.ds(pl.multiple_of(32 + 128 * g + 16 * d, 16), 128), :])
                wide.append(jnp.concatenate(pieces, axis=1))
            inner = jnp.dot(jnp.concatenate(wide, axis=0), amat[0:1280, :], preferred_element_type=F32)
            for par in range(2):
                total = jnp.zeros((8, 16, 128), F32)
                for m in range(LOCAL):
                    term = inner[m * 128 : m * 128 + 128, par * 128 : par * 128 + 128].reshape(8, 16, 128)
                    total = total + own_part(m, par * PAIRS + 8 * g, 8) * term
                ens[pl.ds(par * PAIRS + 8 * g, 8)] = total

            def edge(pair, shifts, at):
                wide = []
                for m in range(LOCAL):
                    wide.append(
                        jnp.concatenate([u[m, 32 + 16 * (pair + d) : 48 + 16 * (pair + d), :] for d in shifts], axis=1)
                    )
                inner = jnp.dot(
                    jnp.concatenate(wide, axis=0), amat[at : at + 768, :], preferred_element_type=F32
                )
                for par in range(2):
                    total = jnp.zeros((1, 16, 128), F32)
                    for m in range(LOCAL):
                        term = inner[m * 16 : m * 16 + 16, par * 128 : par * 128 + 128].reshape(1, 16, 128)
                        total = total + own_part(m, par * PAIRS + pair, 1) * term
                    ens[par * PAIRS + pair : par * PAIRS + pair + 1] = total

            @pl.when(g == 0)
            def _():
                edge(0, range(0, 3), 1280)

            @pl.when(g == 3)
            def _():
                edge(PAIRS - 1, range(-2, 1), 2048)

            even = ens[pl.ds(8 * g, 8)]
            odd = ens[pl.ds(PAIRS + 8 * g, 8)]
            both = jnp.stack([even, odd], axis=1).reshape(QUARTER, 16, 128).astype(BF16)
            es[it, pl.ds(g * QUARTER, QUARTER)] = both

            @pl.when(turn_at < 3)
            def _():
                send_group(it, turn_at)

            return carry

        lax.fori_loop(0, MEMS, group, 0)

    def wait_rs(it):
        wait_bytes(es.at[it], b_recv.at[it])

        @pl.when(to_self)
        def _():
            wait_bytes(es.at[it, 0 : TILES - 1], b_send.at[it])

        @pl.when(jnp.logical_not(to_self))
        def _():
            wait_bytes(es.at[it], b_send.at[it])

        total = rs[it, 0].astype(F32)
        for m in range(1, MEMS):
            total = total + rs[it, m].astype(F32)
        zs[it] = total.astype(BF16)

    def back_copy(it, k):
        return pltpu.make_async_remote_copy(
            src_ref=zs.at[it],
            dst_ref=back.at[it, pl.ds(segment * QUARTER, QUARTER)],
            send_sem=c_send.at[it],
            recv_sem=c_recv.at[it],
            device_id=at_mem(lax.rem(mm + k, MEMS)),
            device_id_type=MESH,
        )

    def start_back(it):
        for k in (2, 1, 3):
            back_copy(it, k).start()
        back[it, pl.ds(segment * QUARTER, QUARTER)] = zs[it]

    def wait_back(it):
        wait_bytes(back.at[it, 0 : 3 * QUARTER], c_recv.at[it])
        wait_bytes(back.at[it, 0 : 3 * QUARTER], c_send.at[it])

    def gather_back(it):
        wide = jnp.concatenate([back[it, 16 * q : 16 * q + 16].reshape(256, 128) for q in range(4)], axis=1)
        for s in range(STENCIL):
            hs[s] = lax.dot_general(
                onehot[s * 512 : s * 512 + 512, :], wide, (((1,), (1,)), ((), ())), preferred_element_type=F32
            ).astype(BF16)

    def prolong(piece):
        total = None
        for s in range(STENCIL):
            term = lax.dot_general(
                hs[s],
                wv[s, piece * 256 : piece * 256 + 256, :],
                (((1,), (1,)), ((), ())),
                preferred_element_type=F32,
            )
            total = term if total is None else total + term
        return total

    loads[9].wait()
    loads[10].wait()
    lax.fori_loop(0, LOCAL, turn, 0)
    pl.semaphore_wait(barrier, TILES - 1 + MEMS - 1)

    def send_halo(m, carry):
        halo_copy(0, m).start()
        halo_copy(1, m).start()
        return carry

    lax.fori_loop(0, LOCAL, send_halo, 0)
    for k in range(1, MEMS):
        pl.semaphore_signal(ready, inc=1, device_id=at_mem(lax.rem(mm + k, MEMS)), device_id_type=MESH)
    for r in range(4):
        loads[r].wait()
        fill_blocks(r, bv[r].astype(BF16))
    loads[4].wait()
    for load in loads[11:]:
        load.wait()
    restrict(0)
    start_c(0)
    for r in range(4):
        loads[5 + r].wait()
    square = jnp.zeros((1, 128), F32)
    diag = jnp.zeros((1, 128), F32)
    for r in range(4):
        v = bv[r]
        square = square + pack_row(v * v)
        diag = diag + pack_row(v * v * (1.0 + sv[r]))
    sum_start(0, 0, stack_rows([square, diag]))
    build()
    wait_halo()
    pl.semaphore_wait(ready, MEMS - 1)
    ensemble(0)

    def col_dot(c_it):
        return pack_row(ens[...] * recv_c[c_it, :, 0:16, :].astype(F32))

    sum_start(1, 0, stack_rows([col_dot(0)]))
    send_group(0, 3)
    sum_start(0, 1, sum_end(0, 0))
    wait_c(0)
    sum_start(1, 1, sum_end(1, 0))
    wait_rs(0)
    start_back(0)
    first_sums = sum_end(0, 1)
    second_sums = sum_end(1, 1)
    rr = pick(first_sums, 0)
    dad = pick(first_sums, 1) + pick(second_sums, 0)
    alpha = rr / dad
    for r in range(4):
        ab[r] = bv[r] * (1.0 + sv[r])
    wait_back(0)
    gather_back(0)
    square = jnp.zeros((1, 128), F32)
    diag = jnp.zeros((1, 128), F32)
    cross = jnp.zeros((1, 128), F32)
    for piece in range(4):
        rr_, half = piece // 2, piece % 2
        total = prolong(piece)
        for p in range(2):
            for q in range(4):
                r = 2 * p + rr_
                cols = slice(q * 512 + half * 256, q * 512 + half * 256 + 256)
                j = 4 * p + q
                d = bv[r, :, cols]
                factor = 1.0 + sv[r, :, cols]
                image = ab[r, :, cols] + total[j * 64 : j * 64 + 64, :]
                ab[r, :, cols] = image
                rnew = d - alpha * image
                fb[j, :, piece * 256 : piece * 256 + 256] = rnew.astype(BF16)
                square = square + pack_row(rnew * rnew)
                diag = diag + pack_row(rnew * rnew * factor)
                cross = cross + pack_row(d * rnew * factor)
    sum_start(2, 0, stack_rows([square, diag, cross]))
    restrict(1)
    start_c(1)
    ensemble(1)
    sum_start(3, 0, stack_rows([col_dot(1), col_dot(0)]))
    send_group(1, 3)
    sum_start(2, 1, sum_end(2, 0))
    wait_c(1)
    sum_start(3, 1, sum_end(3, 0))
    wait_rs(1)
    start_back(1)
    third_sums = sum_end(2, 1)
    fourth_sums = sum_end(3, 1)
    new = pick(third_sums, 0)
    beta = new / rr
    both = pick(third_sums, 2) + pick(fourth_sums, 1)
    dad2 = pick(third_sums, 1) + pick(fourth_sums, 0) + 2.0 * beta * both + beta * beta * dad
    alpha2 = new / dad2
    stores = []
    for r in range(4):
        d = bv[r]
        image = ab[r]
        rnew = d - alpha * image
        outv[0, r] = alpha * d + alpha2 * (rnew + beta * d)
        outv[1, r] = rnew - alpha2 * (rnew * (1.0 + sv[r]) + beta * image)
        stores.append(pltpu.make_async_copy(outv.at[0, r], sol_hbm.at[:, r, :], out_sem.at[r]))
        stores[-1].start()
    wait_back(1)
    gather_back(1)
    for piece in range(4):
        rr_, half = piece // 2, piece % 2
        total = prolong(piece)
        for p in range(2):
            for q in range(4):
                r = 2 * p + rr_
                cols = slice(q * 512 + half * 256, q * 512 + half * 256 + 256)
                j = 4 * p + q
                outv[1, r, :, cols] = outv[1, r, :, cols] - alpha2 * total[j * 64 : j * 64 + 64, :]
        if half == 1:
            for r in (rr_, 2 + rr_):
                stores.append(pltpu.make_async_copy(outv.at[1, r], res_hbm.at[:, r, :], out_sem.at[4 + r]))
                stores[-1].start()
    for store in stores:
        store.wait()


def place(a_ref, b_ref, sol_ref, res_ref, held, in_sems, out_sems):
    reads, writes = [], []
    for part in range(2):
        rows = pl.ds(32 * part, 32)
        for n, (source, target) in enumerate(((a_ref, sol_ref), (b_ref, res_ref))):
            reads.append(pltpu.make_async_copy(source.at[rows], held.at[n, rows], in_sems.at[n, part]))
            writes.append(pltpu.make_async_copy(held.at[n, rows], target.at[rows], out_sems.at[n, part]))
    for read in reads:
        read.start()
    for read, write in zip(reads, writes):
        read.wait()
        write.start()
    for write in writes:
        write.wait()


def on_device(right_side, static_var, members, vertical_root, stencil, weights):
    coef = np.repeat(row_blocks().reshape(44, 4), LEV, axis=1)
    coef = jnp.asarray(np.concatenate([coef, np.zeros((4, 256))]), F32)
    order = np.zeros((ROWS, ROWS))
    for i in range(2):
        for par in range(2):
            for pair in range(PAIRS):
                order[i * 64 + par * PAIRS + pair, 4 * pair + 2 * par + i] = 1.0
    perm = jnp.asarray(order, BF16)
    xop = jnp.asarray(column_operator(), BF16)
    anyspec = pl.BlockSpec(memory_space=pl.ANY)
    field = jax.ShapeDtypeStruct(right_side.shape, F32)
    fields = pl.pallas_call(
        kernel,
        out_shape=(field, field),
        in_specs=[anyspec] * 9,
        out_specs=(anyspec, anyspec),
        scratch_shapes=[
            pltpu.VMEM((LEV, LEV), F32),
            pltpu.VMEM((48, 256), F32),
            pltpu.VMEM((128, 256), BF16),
            pltpu.VMEM((128, 128), BF16),
            pltpu.SMEM((STENCIL, 8), jnp.int32),
            pltpu.VMEM((4, LEV, 2048), F32),
            pltpu.VMEM((4, LEV, 2048), F32),
            pltpu.VMEM((4, LEV, 2048), F32),
            pltpu.VMEM((LOCAL, LEV, WIDTH, 128), BF16),
            pltpu.VMEM((COLS, 128), F32),
            pltpu.VMEM((COLS, 128), F32),
            pltpu.VMEM((2, LOCAL, PAIRS, 16, 128), BF16),
            pltpu.VMEM((2, LOCAL, PAIRS, 16, 128), BF16),
            pltpu.VMEM((LOCAL, TILES, 32, 128), BF16),
            pltpu.VMEM((11 * 256, 256), BF16),
            pltpu.VMEM((STENCIL, 1024, 256), BF16),
            pltpu.VMEM((8, LEV, 1024), BF16),
            pltpu.VMEM((2048, 512), BF16),
            pltpu.VMEM((2, TILES, 32, 128), BF16),
            pltpu.VMEM((2, TILES, 32, 128), BF16),
            pltpu.VMEM((COLS, 128), F32),
            pltpu.VMEM((LOCAL, 576, 256), BF16),
            pltpu.VMEM((TILES, 16, 128), F32),
            pltpu.VMEM((2, TILES, 16, 128), BF16),
            pltpu.VMEM((2, MEMS, QUARTER, 16, 128), BF16),
            pltpu.VMEM((2, QUARTER, 16, 128), BF16),
            pltpu.VMEM((2, TILES, 16, 128), BF16),
            pltpu.VMEM((STENCIL, 512, 256), BF16),
            pltpu.VMEM((2, 4, LEV, 2048), F32),
            pltpu.VMEM((4, 2, 8, 128), F32),
            pltpu.VMEM((4, 2, 16, 8, 128), F32),
            pltpu.SemaphoreType.DMA((15,)),
            pltpu.SemaphoreType.DMA((2,)),
            pltpu.SemaphoreType.DMA((2, 4)),
            pltpu.SemaphoreType.DMA((2,)),
            pltpu.SemaphoreType.DMA((2,)),
            pltpu.SemaphoreType.DMA((2,)),
            pltpu.SemaphoreType.DMA((2,)),
            pltpu.SemaphoreType.DMA((4, 2)),
            pltpu.SemaphoreType.DMA((4, 2)),
            pltpu.SemaphoreType.DMA((2,)),
            pltpu.SemaphoreType.DMA((2,)),
            pltpu.SemaphoreType.REGULAR,
            pltpu.SemaphoreType.DMA((8,)),
        ],
        compiler_params=pltpu.CompilerParams(
            collective_id=0, has_side_effects=True, vmem_limit_bytes=58 * 1024 * 1024
        ),
        name="conjugate_gradient",
    )(right_side, static_var, members, vertical_root, coef, xop, perm, stencil.T, weights)
    return pl.pallas_call(
        place,
        out_shape=(field, field),
        in_specs=[anyspec] * 2,
        out_specs=(anyspec, anyspec),
        scratch_shapes=[
            pltpu.VMEM((2,) + right_side.shape, F32),
            pltpu.SemaphoreType.DMA((2, 8)),
            pltpu.SemaphoreType.DMA((2, 8)),
        ],
        compiler_params=pltpu.CompilerParams(vmem_limit_bytes=58 * 1024 * 1024),
        name="outputs",
    )(*fields)


def solution(mesh):
    in_specs = (
        P(None, "tile", None),
        P(None, "tile", None),
        P("mem", None, "tile", None),
        P(),
        P("tile", None),
        P(),
    )
    out_specs = (P(None, "tile", None), P(None, "tile", None))
    return jax.shard_map(on_device, mesh=mesh, in_specs=in_specs, out_specs=out_specs, check_vma=False)
```
